128 devices in a mesh: dev: 128 (over z, y, x, core).
Axes of the slice: x: 4, y: 4, z: 4, core: 2. Of those that a mesh axis runs over, the one named last changes fastest.
Arguments:
- logits: float32 [32768, 32], P('dev'), may hold values from -8 to 404
- route_cost: float32 [32768, 32], P('dev'), may hold values from 0.1 to 4
- capacity: int32 [8192, 128], P('dev'), may hold values from 0 to 3
- send_route: int32 [128, 128, 64], P('dev'), may hold values from -1 to 8191, as said below
- recv_piece: int32 [4, 128, 128, 64], P(None, 'dev'), may hold values from 0 to 8191, as said below
Outputs:
- demand: float32 [8192, 128], P('dev')
- grad_logits: float32 [32768, 32], P('dev')
The draws below stay inside these ranges and needn't reach their ends.
Inputs may be any that keep to these rules, and one draw needn't show every extreme that they name: `send_route`: the live slots of each block to one owner come first; -1 marks the rest. At most 64 pieces go from one device to one owner; in every draw a few owners, drawn anew, receive exactly 64 from every device. `recv_piece`: slot j of source s's block at owner d describes the piece of send_route's entry (s, d, j): the same route index; first cell plus number of cells is at most 128; empty slots hold four zeros.
All inputs are finite; a program needn't handle non-finite values.
Results may differ from the reference program's by a relative error of at most 0.000037.
Values sent between devices are 32-bit elements; how exact they have to be, the bound alone decides.
No kernel may reach another device: no remote copies, remote signals or barrier semaphores. Data moves between devices by JAX's collectives and lax.ppermute only.
A program may use at most 64 MiB of HBM per device.

```python
import math
import jax
import jax.numpy as jnp

K = 32
TILE_W = 128
TILES_DEV = 64
CAPB = 64
ROUTES_DEV = 8192
NETS = 32768
TILES = 8192
N_DEV = 128


def incidence(key):
    keys = jax.random.split(key, 6)
    order = jax.random.permutation(keys[0], N_DEV)
    popular = order < max(1, N_DEV // 16)
    filled = jax.random.randint(keys[1], (N_DEV, N_DEV), CAPB // 8, CAPB // 2 + 1)
    filled = jnp.where(popular[None, :], CAPB, filled)
    slot_ids = jnp.arange(CAPB, dtype=jnp.int32)
    is_live = slot_ids[None, None, :] < filled[:, :, None]
    shape = (N_DEV, N_DEV, CAPB)
    route_ids = jax.random.randint(keys[2], shape, 0, ROUTES_DEV)
    tile_ids = jax.random.randint(keys[3], shape, 0, TILES_DEV)
    piece_lo = jax.random.randint(keys[4], shape, 0, TILE_W)
    piece_len = jax.random.randint(keys[5], shape, 1, TILE_W + 1 - piece_lo)
    return (is_live, route_ids, tile_ids, piece_lo, piece_len)


def draw_send_route(key, part):
    is_live, route_ids, tile_ids, piece_lo, piece_len = incidence(key)
    return jnp.where(is_live, route_ids, -1).astype(jnp.int32)


def draw_recv_piece(key, part):
    is_live, route_ids, tile_ids, piece_lo, piece_len = incidence(key)
    fields = [jnp.where(is_live, field, 0) for field in (route_ids, tile_ids, piece_lo, piece_len)]
    stacked = jnp.stack(fields, axis=0)
    return jnp.transpose(stacked, (0, 2, 1, 3)).astype(jnp.int32)


def draw_logits(key, part):
    key = jax.random.fold_in(key, 11)
    keys = jax.random.split(key, 1)
    return jnp.clip(2.0 * jax.random.normal(keys[0], (NETS, K), jnp.float32), -8.0, 8.0)


def with_ends(array, key, smallest, high):
    longest = array.shape.index(max(array.shape))
    spots = []
    for shift in (0, 1):
        where = [jax.random.randint(jax.random.fold_in(key, axis), (), 0, length) for axis, length in enumerate(array.shape)]
        where[longest] = (where[longest] + shift) % array.shape[longest]
        spots.append(tuple(where))
    return array.at[spots[0]].set(smallest).at[spots[1]].set(high)


def block_scale(stream_key, extent, cuts, smallest, high):
    def one(dim, blocks):
        heights = jax.random.uniform(jax.random.fold_in(jax.random.fold_in(stream_key, 6), dim), (blocks,), jnp.float32, smallest / len(cuts), high / len(cuts))
        return jnp.repeat(jnp.exp(heights), extent[dim] // blocks).reshape((-1,) + (1,) * (len(extent) - dim - 1))

    level = one(*cuts[0])
    for cut in cuts[1:]:
        level = level * one(*cut)
    return level


def setup_inputs(seed: int = 0) -> dict:
    splits = jax.random.split(jax.random.key(seed), 6)
    logits = draw_logits(jax.random.fold_in(splits[5], 71), 0)
    route_cost = jnp.clip(jnp.exp(math.log(4.0) - 3.6888794 * jax.random.uniform(splits[1], (NETS, K), jnp.float32) ** block_scale(splits[1], (NETS, K), ((0, 128),), -0.2, 0.2)), 0.1, 4.0)
    capacity = with_ends(jax.random.randint(splits[2], (TILES, TILE_W), 0, 4), jax.random.fold_in(splits[2], 1), 0, 3).astype(jnp.int32)
    send_route = draw_send_route(jax.random.fold_in(splits[5], 71), 0)
    recv_piece = draw_recv_piece(jax.random.fold_in(splits[5], 71), 0)
    return dict(logits=logits, route_cost=route_cost, capacity=capacity, send_route=send_route, recv_piece=recv_piece)


SHARPNESS = 2.0


def reference(logits, route_cost, capacity, send_route, recv_piece):
    probabilities = jax.nn.softmax(logits, axis=-1)
    flat_probs = probabilities.reshape(-1)
    route_in = recv_piece[0]
    tile_in = recv_piece[1]
    piece_lo = recv_piece[2]
    piece_len = recv_piece[3]
    owner_ids = jnp.arange(N_DEV, dtype=jnp.int32)[:, None, None]
    source_ids = jnp.arange(N_DEV, dtype=jnp.int32)[None, :, None]
    weight = flat_probs[source_ids * ROUTES_DEV + route_in]
    weight = jnp.where(piece_len > 0, weight, jnp.zeros_like(weight))
    total_cells = TILES * TILE_W
    piece_start = (owner_ids * TILES_DEV + tile_in) * TILE_W + piece_lo
    piece_stop = jnp.where(piece_lo + piece_len < TILE_W, piece_start + piece_len, total_cells).astype(jnp.int32)
    diff_marks = jnp.zeros((total_cells,), jnp.float32)
    diff_marks = diff_marks.at[piece_start.reshape(-1)].add(weight.reshape(-1))
    diff_marks = diff_marks.at[piece_stop.reshape(-1)].add(-weight.reshape(-1), mode="drop")
    demand = jnp.cumsum(diff_marks.reshape(TILES, TILE_W), axis=1)
    pressure = jax.nn.sigmoid(SHARPNESS * (demand - capacity.astype(jnp.float32)))
    prefix = jnp.cumsum(pressure, axis=1).reshape(-1)
    upper_sum = prefix[jnp.clip(piece_start + piece_len - 1, 0, total_cells - 1)]
    lower_sum = jnp.where(piece_lo > 0, prefix[jnp.clip(piece_start - 1, 0, total_cells - 1)], jnp.zeros_like(upper_sum))
    slot_grad = jnp.where(piece_len > 0, upper_sum - lower_sum, jnp.zeros_like(upper_sum))
    per_source = jnp.transpose(slot_grad, (1, 0, 2))
    sender_ids = jnp.arange(N_DEV, dtype=jnp.int32)[:, None, None]
    target_idx = jnp.where(send_route >= 0, sender_ids * ROUTES_DEV + send_route, NETS * K).astype(jnp.int32)
    route_grad = route_cost.reshape(-1).at[target_idx.reshape(-1)].add(per_source.reshape(-1), mode="drop")
    route_grad = route_grad.reshape(NETS, K)
    expected = jnp.sum(probabilities * route_grad, axis=-1, keepdims=True)
    return demand, probabilities * (route_grad - expected)
```

```python
import jax
import jax.numpy as jnp
from jax import lax
from jax.experimental import pallas as pl
from jax.experimental.pallas import tpu as pltpu
from jax.sharding import PartitionSpec as P

SHARPNESS = 2.0
BF = jnp.bfloat16
F32 = jnp.float32
ROWS = 8


def split3(x):
    hi = x.astype(BF)
    rest = x - hi.astype(F32)
    mid = rest.astype(BF)
    low = (rest - mid.astype(F32)).astype(BF)
    return hi, mid, low


def iota_bf(shape):
    return lax.broadcasted_iota(jnp.int32, shape, 0).astype(F32).astype(BF)


def to_bf(x):
    return x.astype(F32).astype(BF)


def one_hot(ids_row, iota):
    ids = jnp.broadcast_to(ids_row, iota.shape)
    return jnp.where(iota == ids, jnp.ones(iota.shape, BF), jnp.zeros(iota.shape, BF))


def gather_kernel(logits_ref, send_ref, weight_ref, prob_ref, held_ref):
    cands, nets = logits_ref.shape
    slots, owners = send_ref.shape
    scores = logits_ref[...]
    powers = jnp.exp(scores - jnp.max(scores, axis=0, keepdims=True))
    probs = powers / jnp.sum(powers, axis=0, keepdims=True)
    prob_ref[...] = probs
    table = jnp.concatenate(split3(probs), axis=0)
    net_iota = iota_bf((nets, owners))
    cand_iota = lax.broadcasted_iota(jnp.int32, (cands, owners), 0)

    def step(i, carry):
        base = pl.multiple_of(i * ROWS, ROWS)
        routes = send_ref[pl.ds(base, ROWS), :]
        net_ids = to_bf(lax.shift_right_arithmetic(routes, 5))
        cand_ids = lax.bitwise_and(routes, 31)
        rows = []
        for j in range(0, ROWS, 2):
            spread = jnp.concatenate(
                [one_hot(net_ids[j + h : j + h + 1], net_iota) for h in range(2)], axis=1
            )
            found = jnp.dot(table, spread, preferred_element_type=F32)
            found = found[:cands] + found[cands : 2 * cands] + found[2 * cands :]
            for h in range(2):
                part = found[:, h * owners : (h + 1) * owners]
                keep = cand_iota == cand_ids[j + h : j + h + 1]
                rows.append(jnp.sum(jnp.where(keep, part, 0.0), axis=0, keepdims=True))
        held_ref[pl.ds(base, ROWS), :] = jnp.concatenate(rows, axis=0)
        return carry

    lax.fori_loop(0, slots // ROWS, step, 0)
    weight_ref[...] = held_ref[...].T


def cells_kernel(weight_ref, piece_ref, capacity_ref, demand_ref, grad_ref, held_ref, total_ref, back_ref):
    slots, sources = held_ref.shape
    tiles, cells = capacity_ref.shape
    held_ref[...] = weight_ref[...].T
    total_ref[...] = jnp.zeros_like(total_ref)
    tile_iota = iota_bf((tiles, sources))
    cell_iota = iota_bf((cells, sources))

    def cover(first_row, stop_row):
        first = jnp.broadcast_to(first_row, cell_iota.shape)
        stop = jnp.broadcast_to(stop_row, cell_iota.shape)
        inside = jnp.logical_and(cell_iota >= first, cell_iota < stop)
        return jnp.where(inside, jnp.ones(cell_iota.shape, BF), jnp.zeros(cell_iota.shape, BF))

    def fields(base):
        tile_ids = to_bf(piece_ref[1, pl.ds(base, ROWS), :])
        first = piece_ref[2, pl.ds(base, ROWS), :]
        stop = first + piece_ref[3, pl.ds(base, ROWS), :]
        return tile_ids, first, stop

    def add(i, carry):
        base = pl.multiple_of(i * ROWS, ROWS)
        tile_ids, first, stop = fields(base)
        first, stop = to_bf(first), to_bf(stop)
        parts = split3(held_ref[pl.ds(base, ROWS), :])
        for j in range(0, ROWS, 2):
            lefts, rights = [], []
            for h in range(2):
                row = slice(j + h, j + h + 1)
                mask = tile_iota == jnp.broadcast_to(tile_ids[row], tile_iota.shape)
                lefts.append(
                    jnp.concatenate(
                        [
                            jnp.where(mask, jnp.broadcast_to(part[row], tile_iota.shape), jnp.zeros(tile_iota.shape, BF))
                            for part in parts
                        ],
                        axis=0,
                    )
                )
                rights.append(cover(first[row], stop[row]))
            total_ref[...] += lax.dot_general(
                jnp.concatenate(lefts, axis=1),
                jnp.concatenate(rights, axis=1),
                (((1,), (1,)), ((), ())),
                preferred_element_type=F32,
            )
        return carry

    lax.fori_loop(0, slots // ROWS, add, 0)
    demand = total_ref[:tiles] + total_ref[tiles : 2 * tiles] + total_ref[2 * tiles :]
    demand_ref[...] = demand
    pressure = jax.nn.sigmoid(SHARPNESS * (demand - capacity_ref[...].astype(F32)))
    table = jnp.concatenate(split3(pressure.T), axis=1)
    wide_iota = lax.broadcasted_iota(jnp.int32, (cells, sources), 0)

    def gather(i, carry):
        base = pl.multiple_of(i * ROWS, ROWS)
        tile_ids, first, stop = fields(base)
        rows = []
        for j in range(0, ROWS, 2):
            spread = []
            for h in range(2):
                hot = one_hot(tile_ids[j + h : j + h + 1], tile_iota)
                spread.append(jnp.concatenate([hot, hot, hot], axis=0))
            found = jnp.dot(table, jnp.concatenate(spread, axis=1), preferred_element_type=F32)
            for h in range(2):
                row = slice(j + h, j + h + 1)
                part = found[:, h * sources : (h + 1) * sources]
                inside = jnp.logical_and(wide_iota >= first[row], wide_iota < stop[row])
                rows.append(jnp.sum(jnp.where(inside, part, 0.0), axis=0, keepdims=True))
        back_ref[pl.ds(base, ROWS), :] = jnp.concatenate(rows, axis=0)
        return carry

    lax.fori_loop(0, slots // ROWS, gather, 0)
    grad_ref[...] = back_ref[...].T


def routes_kernel(grad_ref, send_ref, cost_ref, prob_ref, out_ref, held_ref, total_ref):
    cands, nets = prob_ref.shape
    slots, owners = send_ref.shape
    held_ref[...] = grad_ref[...].T
    total_ref[...] = jnp.zeros_like(total_ref)
    net_iota = iota_bf((nets, owners))
    cand_iota = iota_bf((cands, owners))

    def step(i, carry):
        base = pl.multiple_of(i * ROWS, ROWS)
        routes = send_ref[pl.ds(base, ROWS), :]
        net_ids = to_bf(lax.shift_right_arithmetic(routes, 5))
        cand_ids = to_bf(lax.bitwise_and(routes, 31))
        parts = split3(held_ref[pl.ds(base, ROWS), :])
        for j in range(0, ROWS, 2):
            lefts, rights = [], []
            for h in range(2):
                row = slice(j + h, j + h + 1)
                mask = cand_iota == jnp.broadcast_to(cand_ids[row], cand_iota.shape)
                lefts.append(
                    jnp.concatenate(
                        [
                            jnp.where(mask, jnp.broadcast_to(part[row], cand_iota.shape), jnp.zeros(cand_iota.shape, BF))
                            for part in parts
                        ],
                        axis=0,
                    )
                )
                rights.append(one_hot(net_ids[row], net_iota))
            total_ref[...] += lax.dot_general(
                jnp.concatenate(lefts, axis=1),
                jnp.concatenate(rights, axis=1),
                (((1,), (1,)), ((), ())),
                preferred_element_type=F32,
            )
        return carry

    lax.fori_loop(0, slots // ROWS, step, 0)
    probs = prob_ref[...]
    route_grad = cost_ref[...] + (total_ref[:cands] + total_ref[cands : 2 * cands] + total_ref[2 * cands :])
    expected = jnp.sum(probs * route_grad, axis=0, keepdims=True)
    out_ref[...] = probs * (route_grad - expected)


def in_vmem(count):
    return [pl.BlockSpec(memory_space=pltpu.VMEM)] * count


def body(logits, route_cost, capacity, send_route, recv_piece):
    nets, cands = logits.shape
    tiles, cells = capacity.shape
    send = send_route[0].T
    pieces = jnp.swapaxes(recv_piece[:, 0], 1, 2)
    slots, peers = send.shape
    pairs = jax.ShapeDtypeStruct((peers, slots), F32)
    by_slot = pltpu.VMEM((slots, peers), F32)
    weight, probs = pl.pallas_call(
        gather_kernel,
        out_shape=(pairs, jax.ShapeDtypeStruct((cands, nets), F32)),
        in_specs=in_vmem(2),
        out_specs=tuple(in_vmem(2)),
        scratch_shapes=[by_slot],
    )(logits.T, send)
    weight = lax.all_to_all(weight, "dev", split_axis=0, concat_axis=0, tiled=True)
    demand, slot_grad = pl.pallas_call(
        cells_kernel,
        out_shape=(jax.ShapeDtypeStruct((tiles, cells), F32), pairs),
        in_specs=in_vmem(3),
        out_specs=tuple(in_vmem(2)),
        scratch_shapes=[by_slot, pltpu.VMEM((3 * tiles, cells), F32), by_slot],
    )(weight, pieces, capacity)
    slot_grad = lax.all_to_all(slot_grad, "dev", split_axis=0, concat_axis=0, tiled=True)
    grad = pl.pallas_call(
        routes_kernel,
        out_shape=jax.ShapeDtypeStruct((cands, nets), F32),
        in_specs=in_vmem(4),
        out_specs=pl.BlockSpec(memory_space=pltpu.VMEM),
        scratch_shapes=[by_slot, pltpu.VMEM((3 * cands, nets), F32)],
    )(slot_grad, send, route_cost.T, probs)
    return demand, grad.T


def solution(mesh):
    placed = (
        P("dev", None),
        P("dev", None),
        P("dev", None),
        P("dev", None, None),
        P(None, "dev", None, None),
    )
    return jax.shard_map(
        body,
        mesh=mesh,
        in_specs=placed,
        out_specs=(P("dev", None), P("dev", None)),
        check_vma=False,
    )
```

```python
import jax
import jax.numpy as jnp
from jax import lax
from jax.experimental import pallas as pl
from jax.experimental.pallas import tpu as pltpu
from jax.sharding import PartitionSpec as P

SHARPNESS = 2.0
BF = jnp.bfloat16
F32 = jnp.float32
GATHER_ROWS = 32
CELL_ROWS = 32
ROUTE_ROWS = 64
PARAMS = pltpu.CompilerParams(vmem_limit_bytes=12 * 1024 * 1024)


def split(x):
    high = x.astype(BF)
    return high, (x - high.astype(F32)).astype(BF)


def iota(count, lanes):
    return lax.broadcasted_iota(jnp.int32, (count, lanes), 0)


def to_bf(x):
    return x.astype(F32).astype(BF)


def marks(mask):
    return jnp.where(mask, jnp.ones(mask.shape, BF), jnp.zeros(mask.shape, BF))


def hot(row, places):
    return places == jnp.broadcast_to(row, places.shape)


def spread(row, mask):
    return jnp.where(mask, jnp.broadcast_to(row, mask.shape), jnp.zeros(mask.shape, BF))


def pick(found, row, places):
    return jnp.sum(jnp.where(hot(row, places), found, 0.0), axis=0, keepdims=True)


def contract(left, right):
    return lax.dot_general(left, right, (((1,), (1,)), ((), ())), preferred_element_type=F32)


def route_places(routes, lanes):
    net = lax.shift_right_arithmetic(routes, 5)
    cand = lax.bitwise_and(routes, 31)
    column = lax.bitwise_and(net, lanes - 1)
    row = cand + 32 * lax.shift_right_arithmetic(net, 7)
    return column, row


def fold(x, lanes):
    return jnp.concatenate([x[:, i : i + lanes] for i in range(0, x.shape[1], lanes)], axis=0)


def unfold(x, rows):
    return jnp.concatenate([x[i : i + rows] for i in range(0, x.shape[0], rows)], axis=1)


def gather_kernel(logits_ref, send_ref, weight_ref, prob_ref, held_ref):
    slots, owners = send_ref.shape
    scores = logits_ref[...]
    powers = jnp.exp(scores - jnp.max(scores, axis=0, keepdims=True))
    probs = powers / jnp.sum(powers, axis=0, keepdims=True)
    prob_ref[...] = probs
    folded = fold(probs, owners)
    table = jnp.concatenate(split(folded), axis=1)
    columns = to_bf(iota(owners, owners))
    places = iota(folded.shape[0], owners)

    def step(i, carry):
        base = pl.multiple_of(i * GATHER_ROWS, GATHER_ROWS)
        column, row = route_places(send_ref[pl.ds(base, GATHER_ROWS), :], owners)
        column = to_bf(column)
        hots = jnp.concatenate([marks(hot(column[j : j + 1], columns)) for j in range(GATHER_ROWS)], axis=1)
        found = jnp.dot(table, jnp.concatenate([hots, hots], axis=0), preferred_element_type=F32)
        held_ref[pl.ds(base, GATHER_ROWS), :] = jnp.concatenate(
            [pick(found[:, j * owners : (j + 1) * owners], row[j : j + 1], places) for j in range(GATHER_ROWS)], axis=0
        )
        return carry

    lax.fori_loop(0, slots // GATHER_ROWS, step, 0)
    weight_ref[...] = held_ref[...].T


def cells_kernel(weight_ref, piece_ref, capacity_ref, demand_ref, grad_ref, held_ref, back_ref, cover_ref):
    slots, sources = held_ref.shape
    tiles, cells = capacity_ref.shape
    held_ref[...] = weight_ref[...].T
    tile_places = to_bf(iota(tiles, sources))
    cell_places = to_bf(iota(cells, sources))
    width = CELL_ROWS * sources

    def add(i, total):
        base = pl.multiple_of(i * CELL_ROWS, CELL_ROWS)
        tile = to_bf(piece_ref[1, pl.ds(base, CELL_ROWS), :])
        first = piece_ref[2, pl.ds(base, CELL_ROWS), :]
        stop = to_bf(first + piece_ref[3, pl.ds(base, CELL_ROWS), :])
        first = to_bf(first)
        parts = split(held_ref[pl.ds(base, CELL_ROWS), :])
        lefts, rights = [], []
        for j in range(CELL_ROWS):
            mask = hot(tile[j : j + 1], tile_places)
            lefts.append(jnp.concatenate([spread(part[j : j + 1], mask) for part in parts], axis=0))
            inside = jnp.logical_and(
                cell_places >= jnp.broadcast_to(first[j : j + 1], cell_places.shape),
                cell_places < jnp.broadcast_to(stop[j : j + 1], cell_places.shape),
            )
            rights.append(marks(inside))
        right = jnp.concatenate(rights, axis=1)
        cover_ref[:, pl.ds(pl.multiple_of(i * width, width), width)] = right
        return total + contract(jnp.concatenate(lefts, axis=1), right)

    total = lax.fori_loop(0, slots // CELL_ROWS, add, jnp.zeros((2 * tiles, cells), F32))
    demand = total[:tiles] + total[tiles:]
    demand_ref[...] = demand
    pressure = jax.nn.sigmoid(SHARPNESS * (demand - capacity_ref[...].astype(F32)))
    table = jnp.concatenate(split(pressure), axis=1)
    places = iota(tiles, sources)

    def gather(i, carry):
        base = pl.multiple_of(i * CELL_ROWS, CELL_ROWS)
        tile = piece_ref[1, pl.ds(base, CELL_ROWS), :]
        cover = cover_ref[:, pl.ds(pl.multiple_of(i * width, width), width)]
        found = jnp.dot(table, jnp.concatenate([cover, cover], axis=0), preferred_element_type=F32)
        back_ref[pl.ds(base, CELL_ROWS), :] = jnp.concatenate(
            [pick(found[:, j * sources : (j + 1) * sources], tile[j : j + 1], places) for j in range(CELL_ROWS)], axis=0
        )
        return carry

    lax.fori_loop(0, slots // CELL_ROWS, gather, 0)
    grad_ref[...] = back_ref[...].T


def routes_kernel(grad_ref, send_ref, cost_ref, prob_ref, out_ref, held_ref):
    cands, nets = prob_ref.shape
    slots, owners = send_ref.shape
    rows = cands * nets // owners
    held_ref[...] = grad_ref[...].T
    columns = to_bf(iota(owners, owners))
    places = to_bf(iota(rows, owners))

    def step(i, total):
        base = pl.multiple_of(i * ROUTE_ROWS, ROUTE_ROWS)
        column, row = route_places(send_ref[pl.ds(base, ROUTE_ROWS), :], owners)
        column, row = to_bf(column), to_bf(row)
        parts = split(held_ref[pl.ds(base, ROUTE_ROWS), :])
        lefts, rights = [], []
        for j in range(ROUTE_ROWS):
            mask = hot(row[j : j + 1], places)
            lefts.append(jnp.concatenate([spread(part[j : j + 1], mask) for part in parts], axis=0))
            rights.append(marks(hot(column[j : j + 1], columns)))
        return total + contract(jnp.concatenate(lefts, axis=1), jnp.concatenate(rights, axis=1))

    total = lax.fori_loop(0, slots // ROUTE_ROWS, step, jnp.zeros((2 * rows, owners), F32))
    probs = prob_ref[...]
    route_grad = cost_ref[...] + unfold(total[:rows] + total[rows:], cands)
    expected = jnp.sum(probs * route_grad, axis=0, keepdims=True)
    out_ref[...] = probs * (route_grad - expected)


def in_vmem(count):
    return [pl.BlockSpec(memory_space=pltpu.VMEM)] * count


def gather_call(logits, send):
    cands, nets = logits.shape
    slots, peers = send.shape
    return pl.pallas_call(
        gather_kernel,
        out_shape=(jax.ShapeDtypeStruct((peers, slots), F32), jax.ShapeDtypeStruct((cands, nets), F32)),
        in_specs=in_vmem(2),
        out_specs=tuple(in_vmem(2)),
        compiler_params=PARAMS,
        scratch_shapes=[pltpu.VMEM((slots, peers), F32)],
    )(logits, send)


def cells_call(weight, pieces, capacity):
    tiles, cells = capacity.shape
    peers, slots = weight.shape
    by_slot = pltpu.VMEM((slots, peers), F32)
    return pl.pallas_call(
        cells_kernel,
        out_shape=(jax.ShapeDtypeStruct((tiles, cells), F32), jax.ShapeDtypeStruct((peers, slots), F32)),
        in_specs=in_vmem(3),
        out_specs=tuple(in_vmem(2)),
        compiler_params=PARAMS,
        scratch_shapes=[by_slot, by_slot, pltpu.VMEM((cells, slots * peers), BF)],
    )(weight, pieces, capacity)


def routes_call(slot_grad, send, route_cost, probs):
    return pl.pallas_call(
        routes_kernel,
        out_shape=jax.ShapeDtypeStruct(probs.shape, F32),
        in_specs=in_vmem(4),
        out_specs=pl.BlockSpec(memory_space=pltpu.VMEM),
        compiler_params=PARAMS,
        scratch_shapes=[pltpu.VMEM(send.shape, F32)],
    )(slot_grad, send, route_cost, probs)


def exchange(x):
    return lax.all_to_all(x, "dev", split_axis=0, concat_axis=0, tiled=True)


def body(logits, route_cost, capacity, send_route, recv_piece):
    send = send_route[0].T
    pieces = jnp.swapaxes(recv_piece[:, 0], 1, 2)
    weight, probs = gather_call(logits.T, send)
    demand, slot_grad = cells_call(exchange(weight), pieces, capacity)
    grad = routes_call(exchange(slot_grad), send, route_cost.T, probs)
    return demand, grad.T


def solution(mesh):
    placed = (
        P("dev", None),
        P("dev", None),
        P("dev", None),
        P("dev", None, None),
        P(None, "dev", None, None),
    )
    return jax.shard_map(
        body,
        mesh=mesh,
        in_specs=placed,
        out_specs=(P("dev", None), P("dev", None)),
        check_vma=False,
    )
```

```python
import jax
import jax.numpy as jnp
from jax import lax
from jax.experimental import pallas as pl
from jax.experimental.pallas import tpu as pltpu
from jax.sharding import PartitionSpec as P

SHARPNESS = 2.0
BF = jnp.bfloat16
F32 = jnp.float32
CELL_DOT = 64
CELL_BACK = 4
CELL_BACK_ROWS = 32
CELL_STACK = 1
ROUTE_DOT = 64
SUBLANES = 8
CELL_ROWS = 64
ROUTE_ROWS = 64
PARAMS = pltpu.CompilerParams(vmem_limit_bytes=12 * 1024 * 1024)


def split(x):
    high = x.astype(BF)
    return high, (x - high.astype(F32)).astype(BF)


def iota(count, lanes):
    return lax.broadcasted_iota(jnp.int32, (count, lanes), 0)


def to_bf(x):
    return x.astype(F32).astype(BF)


def marks(mask):
    return jnp.where(mask, jnp.ones(mask.shape, BF), jnp.zeros(mask.shape, BF))


def hot(row, places):
    return places == jnp.broadcast_to(row, places.shape)


def spread(row, mask):
    return jnp.where(mask, jnp.broadcast_to(row, mask.shape), jnp.zeros(mask.shape, BF))


def pick(found, row, places):
    return jnp.sum(jnp.where(hot(row, places), found, 0.0), axis=0, keepdims=True)


def contract(left, right):
    return lax.dot_general(left, right, (((1,), (1,)), ((), ())), preferred_element_type=F32)


def route_places(routes, lanes):
    net = lax.shift_right_arithmetic(routes, 5)
    cand = lax.bitwise_and(routes, 31)
    column = lax.bitwise_and(net, lanes - 1)
    row = cand + 32 * lax.shift_right_arithmetic(net, 7)
    return column, row


def fold(x, lanes):
    return jnp.concatenate([x[:, i : i + lanes] for i in range(0, x.shape[1], lanes)], axis=0)


def unfold(x, rows):
    return jnp.concatenate([x[i : i + rows] for i in range(0, x.shape[0], rows)], axis=1)


def gather_kernel(logits_hbm, send_hbm, weight_ref, prob_ref, logits_ref, send_ref, table_ref, held_ref, sems):
    slots, owners = send_ref.shape
    scores_in = pltpu.make_async_copy(logits_hbm, logits_ref, sems.at[0])
    routes_in = pltpu.make_async_copy(send_hbm, send_ref, sems.at[1])
    scores_in.start()
    routes_in.start()
    scores_in.wait()
    scores = logits_ref[...]
    powers = jnp.exp(scores - jnp.max(scores, axis=0, keepdims=True))
    probs = powers / jnp.sum(powers, axis=0, keepdims=True)
    prob_ref[...] = probs
    table_ref[...] = fold(probs, owners)
    routes_in.wait()
    column, row = route_places(send_ref[...], owners)
    blocks = range(0, slots, SUBLANES)
    shape = (SUBLANES, owners)
    columns = [column[i : i + SUBLANES] for i in blocks]
    rows = [row[i : i + SUBLANES] for i in blocks]

    def take(t, n, found):
        entries = jnp.broadcast_to(table_ref[t : t + 1, :], shape)
        entries = jnp.take_along_axis(entries, columns[n], axis=1, mode="promise_in_bounds")
        return jnp.where(rows[n] == t, entries, found)

    founds = [jnp.zeros(shape, F32) for _ in blocks]
    for n in range(len(founds)):
        for t in range(table_ref.shape[0]):
            founds[n] = take(t, n, founds[n])
    for n, i in enumerate(blocks):
        held_ref[i : i + SUBLANES, :] = founds[n]
    weight_ref[...] = held_ref[...].T


def cells_kernel(weight_ref, piece_ref, capacity_ref, demand_hbm, grad_ref, held_ref, back_ref, cover_ref, demand_ref, sem):
    slots, sources = held_ref.shape
    tiles, cells = capacity_ref.shape
    held_ref[...] = weight_ref[...].T
    tile_places = to_bf(iota(tiles, sources))
    cell_places = to_bf(iota(cells, sources))
    width = CELL_ROWS * sources

    def add(i, total):
        base = pl.multiple_of(i * CELL_ROWS, CELL_ROWS)
        tile = to_bf(piece_ref[1, pl.ds(base, CELL_ROWS), :])
        first = piece_ref[2, pl.ds(base, CELL_ROWS), :]
        stop = to_bf(first + piece_ref[3, pl.ds(base, CELL_ROWS), :])
        first = to_bf(first)
        parts = split(held_ref[pl.ds(base, CELL_ROWS), :])
        for k in range(0, CELL_ROWS, CELL_DOT):
            lefts, rights = [], []
            for j in range(k, k + CELL_DOT):
                mask = hot(tile[j : j + 1], tile_places)
                lefts.append(jnp.concatenate([spread(part[j : j + 1], mask) for part in parts], axis=0))
                inside = jnp.logical_and(
                    cell_places >= jnp.broadcast_to(first[j : j + 1], cell_places.shape),
                    cell_places < jnp.broadcast_to(stop[j : j + 1], cell_places.shape),
                )
                rights.append(marks(inside))
                cover_ref[:, pl.ds(pl.multiple_of(i * width + j * sources, sources), sources)] = rights[-1]
            total = total + contract(jnp.concatenate(lefts, axis=1), jnp.concatenate(rights, axis=1))
        return total

    total = lax.fori_loop(0, slots // CELL_ROWS, add, jnp.zeros((2 * tiles, cells), F32))
    demand = total[:tiles] + total[tiles:]
    demand_ref[...] = demand
    demand_out = pltpu.make_async_copy(demand_ref, demand_hbm, sem)
    demand_out.start()
    pressure = jax.nn.sigmoid(SHARPNESS * (demand - capacity_ref[...].astype(F32)))
    table = jnp.concatenate(split(pressure), axis=1 - CELL_STACK)
    places = iota(tiles, sources)

    def gather(i, carry):
        base = pl.multiple_of(i * CELL_BACK_ROWS, CELL_BACK_ROWS)
        tile = piece_ref[1, pl.ds(base, CELL_BACK_ROWS), :]
        picked = []
        for k in range(0, CELL_BACK_ROWS, CELL_BACK):
            cover = cover_ref[:, pl.ds(pl.multiple_of((base + k) * sources, sources), CELL_BACK * sources)]
            if CELL_STACK:
                found = jnp.dot(table, cover, preferred_element_type=F32)
                found = found[:tiles] + found[tiles:]
            else:
                found = jnp.dot(table, jnp.concatenate([cover, cover], axis=0), preferred_element_type=F32)
            picked += [pick(found[:, (j - k) * sources : (j - k + 1) * sources], tile[j : j + 1], places) for j in range(k, k + CELL_BACK)]
        back_ref[pl.ds(base, CELL_BACK_ROWS), :] = jnp.concatenate(picked, axis=0)
        return carry

    lax.fori_loop(0, slots // CELL_BACK_ROWS, gather, 0)
    grad_ref[...] = back_ref[...].T
    demand_out.wait()


def routes_kernel(grad_ref, send_ref, cost_ref, prob_ref, out_ref, held_ref):
    cands, nets = prob_ref.shape
    slots, owners = send_ref.shape
    rows = cands * nets // owners
    held_ref[...] = grad_ref[...].T
    columns = to_bf(iota(owners, owners))
    places = to_bf(iota(rows, owners))

    def step(i, total):
        base = pl.multiple_of(i * ROUTE_ROWS, ROUTE_ROWS)
        column, row = route_places(send_ref[pl.ds(base, ROUTE_ROWS), :], owners)
        column, row = to_bf(column), to_bf(row)
        parts = split(held_ref[pl.ds(base, ROUTE_ROWS), :])
        for k in range(0, ROUTE_ROWS, ROUTE_DOT):
            lefts, rights = [], []
            for j in range(k, k + ROUTE_DOT):
                mask = hot(row[j : j + 1], places)
                lefts.append(jnp.concatenate([spread(part[j : j + 1], mask) for part in parts], axis=0))
                rights.append(marks(hot(column[j : j + 1], columns)))
            total = total + contract(jnp.concatenate(lefts, axis=1), jnp.concatenate(rights, axis=1))
        return total

    total = lax.fori_loop(0, slots // ROUTE_ROWS, step, jnp.zeros((2 * rows, owners), F32))
    probs = prob_ref[...]
    route_grad = cost_ref[...] + unfold(total[:rows] + total[rows:], cands)
    expected = jnp.sum(probs * route_grad, axis=0, keepdims=True)
    out_ref[...] = probs * (route_grad - expected)


def in_vmem(count):
    return [pl.BlockSpec(memory_space=pltpu.VMEM)] * count


def in_hbm(count):
    return [pl.BlockSpec(memory_space=pltpu.HBM)] * count


def gather_call(logits, send):
    cands, nets = logits.shape
    slots, peers = send.shape
    return pl.pallas_call(
        gather_kernel,
        out_shape=(jax.ShapeDtypeStruct((peers, slots), F32), jax.ShapeDtypeStruct((cands, nets), F32)),
        in_specs=in_hbm(2),
        out_specs=tuple(in_vmem(2)),
        compiler_params=PARAMS,
        scratch_shapes=[
            pltpu.VMEM((cands, nets), F32),
            pltpu.VMEM((slots, peers), jnp.int32),
            pltpu.VMEM((cands * nets // peers, peers), F32),
            pltpu.VMEM((slots, peers), F32),
            pltpu.SemaphoreType.DMA((2,)),
        ],
    )(logits, send)


def cells_call(weight, pieces, capacity):
    tiles, cells = capacity.shape
    peers, slots = weight.shape
    by_slot = pltpu.VMEM((slots, peers), F32)
    return pl.pallas_call(
        cells_kernel,
        out_shape=(jax.ShapeDtypeStruct((tiles, cells), F32), jax.ShapeDtypeStruct((peers, slots), F32)),
        in_specs=in_vmem(3),
        out_specs=tuple(in_hbm(1) + in_vmem(1)),
        compiler_params=PARAMS,
        scratch_shapes=[
            by_slot,
            by_slot,
            pltpu.VMEM((cells, slots * peers), BF),
            pltpu.VMEM((tiles, cells), F32),
            pltpu.SemaphoreType.DMA,
        ],
    )(weight, pieces, capacity)


def routes_call(slot_grad, send, route_cost, probs):
    return pl.pallas_call(
        routes_kernel,
        out_shape=jax.ShapeDtypeStruct(probs.shape, F32),
        in_specs=in_vmem(4),
        out_specs=pl.BlockSpec(memory_space=pltpu.VMEM),
        compiler_params=PARAMS,
        scratch_shapes=[pltpu.VMEM(send.shape, F32)],
    )(slot_grad, send, route_cost, probs)


def exchange(x):
    return lax.all_to_all(x, "dev", split_axis=0, concat_axis=0, tiled=True)


def body(logits, route_cost, capacity, send_route, recv_piece):
    send = send_route[0].T
    pieces = jnp.swapaxes(recv_piece[:, 0], 1, 2)
    weight, probs = gather_call(logits.T, send)
    demand, slot_grad = cells_call(exchange(weight), pieces, capacity)
    grad = routes_call(exchange(slot_grad), send, route_cost.T, probs)
    return demand, grad.T


def solution(mesh):
    placed = (
        P("dev", None),
        P("dev", None),
        P("dev", None),
        P("dev", None, None),
        P(None, "dev", None, None),
    )
    return jax.shard_map(
        body,
        mesh=mesh,
        in_specs=placed,
        out_specs=(P("dev", None), P("dev", None)),
        check_vma=False,
    )
```

```python
import jax
import jax.numpy as jnp
from jax import lax
from jax.experimental import pallas as pl
from jax.experimental.pallas import tpu as pltpu
from jax.sharding import PartitionSpec as P

SHARPNESS = 2.0
BF = jnp.bfloat16
F32 = jnp.float32
CELL_DOT = 64
CELL_BACK = 4
CELL_BACK_ROWS = 32
CELL_STACK = 1
ROUTE_DOT = 64
SUBLANES = 8
CELL_ROWS = 64
ROUTE_ROWS = 64
PARAMS = pltpu.CompilerParams(vmem_limit_bytes=12 * 1024 * 1024)


def split(x):
    high = x.astype(BF)
    return high, (x - high.astype(F32)).astype(BF)


def iota(count, lanes):
    return lax.broadcasted_iota(jnp.int32, (count, lanes), 0)


def to_bf(x):
    return x.astype(F32).astype(BF)


def marks(mask):
    return jnp.where(mask, jnp.ones(mask.shape, BF), jnp.zeros(mask.shape, BF))


def hot(row, places):
    return places == jnp.broadcast_to(row, places.shape)


def spread(row, mask):
    return jnp.where(mask, jnp.broadcast_to(row, mask.shape), jnp.zeros(mask.shape, BF))


def pick(found, row, places):
    return jnp.sum(jnp.where(hot(row, places), found, 0.0), axis=0, keepdims=True)


def contract(left, right):
    return lax.dot_general(left, right, (((1,), (1,)), ((), ())), preferred_element_type=F32)


def route_places(routes, lanes):
    net = lax.shift_right_arithmetic(routes, 5)
    cand = lax.bitwise_and(routes, 31)
    column = lax.bitwise_and(net, lanes - 1)
    row = cand + 32 * lax.shift_right_arithmetic(net, 7)
    return column, row


def fold(x, lanes):
    return jnp.concatenate([x[:, i : i + lanes] for i in range(0, x.shape[1], lanes)], axis=0)


def unfold(x, rows):
    return jnp.concatenate([x[i : i + rows] for i in range(0, x.shape[0], rows)], axis=1)


def gather_kernel(logits_hbm, send_hbm, weight_ref, prob_ref, logits_ref, send_ref, table_ref, held_ref, sems):
    slots, owners = send_ref.shape
    scores_in = pltpu.make_async_copy(logits_hbm, logits_ref, sems.at[0])
    routes_in = pltpu.make_async_copy(send_hbm, send_ref, sems.at[1])
    scores_in.start()
    routes_in.start()
    scores_in.wait()
    scores = logits_ref[...]
    powers = jnp.exp(scores - jnp.max(scores, axis=0, keepdims=True))
    probs = powers / jnp.sum(powers, axis=0, keepdims=True)
    prob_ref[...] = probs
    table_ref[...] = fold(probs, owners)
    routes_in.wait()
    column, row = route_places(send_ref[...], owners)
    blocks = range(0, slots, SUBLANES)
    shape = (SUBLANES, owners)
    columns = [column[i : i + SUBLANES] for i in blocks]
    rows = [row[i : i + SUBLANES] for i in blocks]

    def take(t, n, found):
        entries = jnp.broadcast_to(table_ref[t : t + 1, :], shape)
        entries = jnp.take_along_axis(entries, columns[n], axis=1, mode="promise_in_bounds")
        return jnp.where(rows[n] == t, entries, found)

    founds = [jnp.zeros(shape, F32) for _ in blocks]
    for n in range(len(founds)):
        for t in range(table_ref.shape[0]):
            founds[n] = take(t, n, founds[n])
    for n, i in enumerate(blocks):
        held_ref[i : i + SUBLANES, :] = founds[n]
    weight_ref[...] = held_ref[...].T


def cells_kernel(weight_ref, piece_ref, capacity_ref, demand_hbm, grad_ref, held_ref, back_ref, cover_ref, demand_ref, sem):
    slots, sources = held_ref.shape
    tiles, cells = capacity_ref.shape
    held_ref[...] = weight_ref[...].T
    tile_places = to_bf(iota(tiles, sources))
    cell_places = to_bf(iota(cells, sources))
    width = CELL_ROWS * sources

    def add(i, total):
        base = pl.multiple_of(i * CELL_ROWS, CELL_ROWS)
        tile = to_bf(piece_ref[1, pl.ds(base, CELL_ROWS), :])
        first = piece_ref[2, pl.ds(base, CELL_ROWS), :]
        stop = to_bf(first + piece_ref[3, pl.ds(base, CELL_ROWS), :])
        first = to_bf(first)
        parts = split(held_ref[pl.ds(base, CELL_ROWS), :])
        for k in range(0, CELL_ROWS, CELL_DOT):
            lefts, rights = [], []
            for j in range(k, k + CELL_DOT):
                mask = hot(tile[j : j + 1], tile_places)
                lefts.append(jnp.concatenate([spread(part[j : j + 1], mask) for part in parts], axis=0))
                inside = jnp.logical_and(
                    cell_places >= jnp.broadcast_to(first[j : j + 1], cell_places.shape),
                    cell_places < jnp.broadcast_to(stop[j : j + 1], cell_places.shape),
                )
                rights.append(marks(inside))
                cover_ref[:, pl.ds(pl.multiple_of(i * width + j * sources, sources), sources)] = rights[-1]
            total = total + contract(jnp.concatenate(lefts, axis=1), jnp.concatenate(rights, axis=1))
        return total

    total = lax.fori_loop(0, slots // CELL_ROWS, add, jnp.zeros((2 * tiles, cells), F32))
    demand = total[:tiles] + total[tiles:]
    demand_ref[...] = demand
    demand_out = pltpu.make_async_copy(demand_ref, demand_hbm, sem)
    demand_out.start()
    pressure = jax.nn.sigmoid(SHARPNESS * (demand - capacity_ref[...].astype(F32)))
    table = jnp.concatenate(split(pressure), axis=1 - CELL_STACK)
    places = iota(tiles, sources)

    def gather(i, carry):
        base = pl.multiple_of(i * CELL_BACK_ROWS, CELL_BACK_ROWS)
        tile = piece_ref[1, pl.ds(base, CELL_BACK_ROWS), :]
        picked = []
        for k in range(0, CELL_BACK_ROWS, CELL_BACK):
            cover = cover_ref[:, pl.ds(pl.multiple_of((base + k) * sources, sources), CELL_BACK * sources)]
            if CELL_STACK:
                found = jnp.dot(table, cover, preferred_element_type=F32)
                found = found[:tiles] + found[tiles:]
            else:
                found = jnp.dot(table, jnp.concatenate([cover, cover], axis=0), preferred_element_type=F32)
            picked += [pick(found[:, (j - k) * sources : (j - k + 1) * sources], tile[j : j + 1], places) for j in range(k, k + CELL_BACK)]
        back_ref[pl.ds(base, CELL_BACK_ROWS), :] = jnp.concatenate(picked, axis=0)
        return carry

    lax.fori_loop(0, slots // CELL_BACK_ROWS, gather, 0)
    grad_ref[...] = back_ref[...].T
    demand_out.wait()


def routes_kernel(grad_ref, send_ref, cost_ref, prob_ref, out_ref, held_ref):
    cands, nets = prob_ref.shape
    slots, owners = send_ref.shape
    rows = cands * nets // owners
    held_ref[...] = grad_ref[...].T
    columns = to_bf(iota(owners, owners))
    places = to_bf(iota(rows, owners))

    def step(i, total):
        base = pl.multiple_of(i * ROUTE_ROWS, ROUTE_ROWS)
        column, row = route_places(send_ref[pl.ds(base, ROUTE_ROWS), :], owners)
        column, row = to_bf(column), to_bf(row)
        parts = split(held_ref[pl.ds(base, ROUTE_ROWS), :])
        for k in range(0, ROUTE_ROWS, ROUTE_DOT):
            lefts, rights = [], []
            for j in range(k, k + ROUTE_DOT):
                mask = hot(row[j : j + 1], places)
                lefts.append(jnp.concatenate([spread(part[j : j + 1], mask) for part in parts], axis=0))
                rights.append(marks(hot(column[j : j + 1], columns)))
            total = total + contract(jnp.concatenate(lefts, axis=1), jnp.concatenate(rights, axis=1))
        return total

    total = lax.fori_loop(0, slots // ROUTE_ROWS, step, jnp.zeros((2 * rows, owners), F32))
    probs = prob_ref[...]
    route_grad = cost_ref[...] + unfold(total[:rows] + total[rows:], cands)
    expected = jnp.sum(probs * route_grad, axis=0, keepdims=True)
    out_ref[...] = probs * (route_grad - expected)


def in_vmem(count):
    return [pl.BlockSpec(memory_space=pltpu.VMEM)] * count


def in_hbm(count):
    return [pl.BlockSpec(memory_space=pltpu.HBM)] * count


def gather_call(logits, send):
    cands, nets = logits.shape
    slots, peers = send.shape
    return pl.pallas_call(
        gather_kernel,
        out_shape=(jax.ShapeDtypeStruct((peers, slots), F32), jax.ShapeDtypeStruct((cands, nets), F32)),
        in_specs=in_hbm(2),
        out_specs=tuple(in_vmem(2)),
        compiler_params=PARAMS,
        scratch_shapes=[
            pltpu.VMEM((cands, nets), F32),
            pltpu.VMEM((slots, peers), jnp.int32),
            pltpu.VMEM((cands * nets // peers, peers), F32),
            pltpu.VMEM((slots, peers), F32),
            pltpu.SemaphoreType.DMA((2,)),
        ],
    )(*[pltpu.with_memory_space_constraint(x, pltpu.HBM) for x in (logits, send)])


def cells_call(weight, pieces, capacity):
    tiles, cells = capacity.shape
    peers, slots = weight.shape
    by_slot = pltpu.VMEM((slots, peers), F32)
    return pl.pallas_call(
        cells_kernel,
        out_shape=(jax.ShapeDtypeStruct((tiles, cells), F32), jax.ShapeDtypeStruct((peers, slots), F32)),
        in_specs=in_vmem(3),
        out_specs=tuple(in_hbm(1) + in_vmem(1)),
        compiler_params=PARAMS,
        scratch_shapes=[
            by_slot,
            by_slot,
            pltpu.VMEM((cells, slots * peers), BF),
            pltpu.VMEM((tiles, cells), F32),
            pltpu.SemaphoreType.DMA,
        ],
    )(weight, pieces, capacity)


def routes_call(slot_grad, send, route_cost, probs):
    return pl.pallas_call(
        routes_kernel,
        out_shape=jax.ShapeDtypeStruct(probs.shape, F32),
        in_specs=in_vmem(4),
        out_specs=pl.BlockSpec(memory_space=pltpu.VMEM),
        compiler_params=PARAMS,
        scratch_shapes=[pltpu.VMEM(send.shape, F32)],
    )(slot_grad, send, route_cost, probs)


def exchange(x):
    return lax.all_to_all(x, "dev", split_axis=0, concat_axis=0, tiled=True)


def body(logits, route_cost, capacity, send_route, recv_piece):
    send = send_route[0].T
    pieces = jnp.swapaxes(recv_piece[:, 0], 1, 2)
    weight, probs = gather_call(logits.T, send)
    demand, slot_grad = cells_call(exchange(weight), pieces, capacity)
    grad = routes_call(exchange(slot_grad), send, route_cost.T, probs)
    return demand, grad.T


def solution(mesh):
    placed = (
        P("dev", None),
        P("dev", None),
        P("dev", None),
        P("dev", None, None),
        P(None, "dev", None, None),
    )
    return jax.shard_map(
        body,
        mesh=mesh,
        in_specs=placed,
        out_specs=(P("dev", None), P("dev", None)),
        check_vma=False,
    )
```

```python
import jax
import jax.numpy as jnp
from jax import lax
from jax.experimental import pallas as pl
from jax.experimental.pallas import tpu as pltpu
from jax.sharding import PartitionSpec as P

SHARPNESS = 2.0
BF = jnp.bfloat16
F32 = jnp.float32
CELL_DOT = 64
CELL_BACK = 4
CELL_BACK_ROWS = 32
ROUTE_DOT = 64
SUBLANES = 8
BY_PRODUCT = 32
GATHER_DOT = 8
CELL_ROWS = 64
ROUTE_ROWS = 64
PARAMS = pltpu.CompilerParams(vmem_limit_bytes=12 * 1024 * 1024)


def split(x):
    high = x.astype(BF)
    return high, (x - high.astype(F32)).astype(BF)


def iota(count, lanes):
    return lax.broadcasted_iota(jnp.int32, (count, lanes), 0)


def to_bf(x):
    return x.astype(F32).astype(BF)


def marks(mask):
    return jnp.where(mask, jnp.ones(mask.shape, BF), jnp.zeros(mask.shape, BF))


def hot(row, places):
    return places == jnp.broadcast_to(row, places.shape)


def spread(row, mask):
    return jnp.where(mask, jnp.broadcast_to(row, mask.shape), jnp.zeros(mask.shape, BF))


def pick(found, row, places):
    return jnp.sum(jnp.where(hot(row, places), found, 0.0), axis=0, keepdims=True)


def contract(left, right):
    return lax.dot_general(left, right, (((1,), (1,)), ((), ())), preferred_element_type=F32)


def route_places(routes, lanes):
    net = lax.shift_right_arithmetic(routes, 5)
    cand = lax.bitwise_and(routes, 31)
    column = lax.bitwise_and(net, lanes - 1)
    row = cand + 32 * lax.shift_right_arithmetic(net, 7)
    return column, row


def fold(x, lanes):
    return jnp.concatenate([x[:, i : i + lanes] for i in range(0, x.shape[1], lanes)], axis=0)


def unfold(x, rows):
    return jnp.concatenate([x[i : i + rows] for i in range(0, x.shape[0], rows)], axis=1)


def lane_gather(table_ref, place, lanes):
    stack = []
    for t in range(table_ref.shape[0]):
        entries = jnp.broadcast_to(table_ref[t : t + 1, :], lanes.shape)
        found = jnp.take_along_axis(entries, lanes, axis=1, mode="promise_in_bounds")
        depth = 0
        while stack and stack[-1][1] == depth:
            found = jnp.where(lax.bitwise_and(place, 1 << depth) != 0, found, stack.pop()[0])
            depth += 1
        stack.append((found, depth))
    return stack[0][0]


def gather_kernel(logits_hbm, send_hbm, weight_ref, prob_ref, logits_ref, send_ref, table_ref, held_ref, sems):
    slots, owners = send_ref.shape
    scores_in = pltpu.make_async_copy(logits_hbm, logits_ref, sems.at[0])
    routes_in = pltpu.make_async_copy(send_hbm, send_ref, sems.at[1])
    scores_in.start()
    routes_in.start()
    scores_in.wait()
    scores = logits_ref[...]
    powers = jnp.exp(scores - jnp.max(scores, axis=0, keepdims=True))
    probs = powers / jnp.sum(powers, axis=0, keepdims=True)
    prob_ref[...] = probs
    table_ref[...] = fold(probs, owners)
    routes_in.wait()
    column, row = route_places(send_ref[...], owners)
    high = table_ref.shape[0]
    cut = slots - BY_PRODUCT
    folded = table_ref[...]
    parts = jnp.concatenate(split(folded), axis=0)
    column_bf = to_bf(column[cut:])
    column_places = to_bf(iota(owners, owners))
    places = iota(high, owners)
    picked = []
    for k in range(0, BY_PRODUCT, GATHER_DOT):
        hots = [marks(hot(column_bf[j : j + 1], column_places)) for j in range(k, k + GATHER_DOT)]
        found = jnp.dot(parts, jnp.concatenate(hots, axis=1), preferred_element_type=F32)
        found = found[:high] + found[high:]
        for j in range(k, k + GATHER_DOT):
            part = found[:, (j - k) * owners : (j - k + 1) * owners]
            picked.append(pick(part, row[cut + j : cut + j + 1], places))
    held_ref[cut:, :] = jnp.concatenate(picked, axis=0)
    for base in range(0, cut, SUBLANES):
        lanes, place = column[base : base + SUBLANES], row[base : base + SUBLANES]
        found = lane_gather(table_ref, place, lanes)
        held_ref[base : base + SUBLANES, :] = jnp.where(place >= 0, found, 0.0)
    weight_ref[...] = held_ref[...].T


def cells_kernel(weight_ref, piece_ref, capacity_ref, demand_hbm, grad_ref, held_ref, back_ref, cover_ref, demand_ref, sem):
    slots, sources = held_ref.shape
    tiles, cells = capacity_ref.shape
    held_ref[...] = weight_ref[...].T
    tile_places = to_bf(iota(tiles, sources))
    cell_places = to_bf(iota(cells, sources))
    width = CELL_ROWS * sources

    def add(i, total):
        base = pl.multiple_of(i * CELL_ROWS, CELL_ROWS)
        tile = to_bf(piece_ref[1, pl.ds(base, CELL_ROWS), :])
        first = piece_ref[2, pl.ds(base, CELL_ROWS), :]
        stop = to_bf(first + piece_ref[3, pl.ds(base, CELL_ROWS), :])
        first = to_bf(first)
        parts = split(held_ref[pl.ds(base, CELL_ROWS), :])
        for k in range(0, CELL_ROWS, CELL_DOT):
            lefts, rights = [], []
            for j in range(k, k + CELL_DOT):
                mask = hot(tile[j : j + 1], tile_places)
                lefts.append(jnp.concatenate([spread(part[j : j + 1], mask) for part in parts], axis=0))
                inside = jnp.logical_and(
                    cell_places >= jnp.broadcast_to(first[j : j + 1], cell_places.shape),
                    cell_places < jnp.broadcast_to(stop[j : j + 1], cell_places.shape),
                )
                rights.append(marks(inside))
                cover_ref[:, pl.ds(pl.multiple_of(i * width + j * sources, sources), sources)] = rights[-1]
            total = total + contract(jnp.concatenate(lefts, axis=1), jnp.concatenate(rights, axis=1))
        return total

    total = lax.fori_loop(0, slots // CELL_ROWS, add, jnp.zeros((2 * tiles, cells), F32))
    demand = total[:tiles] + total[tiles:]
    demand_ref[...] = demand
    demand_out = pltpu.make_async_copy(demand_ref, demand_hbm, sem)
    demand_out.start()
    pressure = jax.nn.sigmoid(SHARPNESS * (demand - capacity_ref[...].astype(F32)))
    table = jnp.concatenate(split(pressure), axis=0)
    places = iota(tiles, sources)

    def gather(i, carry):
        base = pl.multiple_of(i * CELL_BACK_ROWS, CELL_BACK_ROWS)
        tile = piece_ref[1, pl.ds(base, CELL_BACK_ROWS), :]
        picked = []
        for k in range(0, CELL_BACK_ROWS, CELL_BACK):
            cover = cover_ref[:, pl.ds(pl.multiple_of((base + k) * sources, sources), CELL_BACK * sources)]
            found = jnp.dot(table, cover, preferred_element_type=F32)
            found = found[:tiles] + found[tiles:]
            for j in range(k, k + CELL_BACK):
                part = found[:, (j - k) * sources : (j - k + 1) * sources]
                picked.append(pick(part, tile[j : j + 1], places))
        back_ref[pl.ds(base, CELL_BACK_ROWS), :] = jnp.concatenate(picked, axis=0)
        return carry

    lax.fori_loop(0, slots // CELL_BACK_ROWS, gather, 0)
    grad_ref[...] = back_ref[...].T
    demand_out.wait()


def routes_kernel(grad_ref, send_ref, cost_ref, prob_ref, out_ref, held_ref):
    cands, nets = prob_ref.shape
    slots, owners = send_ref.shape
    rows = cands * nets // owners
    held_ref[...] = grad_ref[...].T
    columns = to_bf(iota(owners, owners))
    places = to_bf(iota(rows, owners))

    def step(i, total):
        base = pl.multiple_of(i * ROUTE_ROWS, ROUTE_ROWS)
        column, row = route_places(send_ref[pl.ds(base, ROUTE_ROWS), :], owners)
        column, row = to_bf(column), to_bf(row)
        parts = split(held_ref[pl.ds(base, ROUTE_ROWS), :])
        for k in range(0, ROUTE_ROWS, ROUTE_DOT):
            lefts, rights = [], []
            for j in range(k, k + ROUTE_DOT):
                mask = hot(row[j : j + 1], places)
                lefts.append(jnp.concatenate([spread(part[j : j + 1], mask) for part in parts], axis=0))
                rights.append(marks(hot(column[j : j + 1], columns)))
            total = total + contract(jnp.concatenate(lefts, axis=1), jnp.concatenate(rights, axis=1))
        return total

    total = lax.fori_loop(0, slots // ROUTE_ROWS, step, jnp.zeros((2 * rows, owners), F32))
    probs = prob_ref[...]
    route_grad = cost_ref[...] + unfold(total[:rows] + total[rows:], cands)
    expected = jnp.sum(probs * route_grad, axis=0, keepdims=True)
    out_ref[...] = probs * (route_grad - expected)


def in_vmem(count):
    return [pl.BlockSpec(memory_space=pltpu.VMEM)] * count


def in_hbm(count):
    return [pl.BlockSpec(memory_space=pltpu.HBM)] * count


def gather_call(logits, send):
    cands, nets = logits.shape
    slots, peers = send.shape
    return pl.pallas_call(
        gather_kernel,
        out_shape=(jax.ShapeDtypeStruct((peers, slots), F32), jax.ShapeDtypeStruct((cands, nets), F32)),
        in_specs=in_hbm(2),
        out_specs=tuple(in_vmem(2)),
        compiler_params=PARAMS,
        scratch_shapes=[
            pltpu.VMEM((cands, nets), F32),
            pltpu.VMEM((slots, peers), jnp.int32),
            pltpu.VMEM((cands * nets // peers, peers), F32),
            pltpu.VMEM((slots, peers), F32),
            pltpu.SemaphoreType.DMA((2,)),
        ],
    )(*[pltpu.with_memory_space_constraint(x, pltpu.HBM) for x in (logits, send)])


def cells_call(weight, pieces, capacity):
    tiles, cells = capacity.shape
    peers, slots = weight.shape
    by_slot = pltpu.VMEM((slots, peers), F32)
    return pl.pallas_call(
        cells_kernel,
        out_shape=(jax.ShapeDtypeStruct((tiles, cells), F32), jax.ShapeDtypeStruct((peers, slots), F32)),
        in_specs=in_vmem(3),
        out_specs=tuple(in_hbm(1) + in_vmem(1)),
        compiler_params=PARAMS,
        scratch_shapes=[
            by_slot,
            by_slot,
            pltpu.VMEM((cells, slots * peers), BF),
            pltpu.VMEM((tiles, cells), F32),
            pltpu.SemaphoreType.DMA,
        ],
    )(weight, pieces, capacity)


def routes_call(slot_grad, send, route_cost, probs):
    return pl.pallas_call(
        routes_kernel,
        out_shape=jax.ShapeDtypeStruct(probs.shape, F32),
        in_specs=in_vmem(4),
        out_specs=pl.BlockSpec(memory_space=pltpu.VMEM),
        compiler_params=PARAMS,
        scratch_shapes=[pltpu.VMEM(send.shape, F32)],
    )(slot_grad, send, route_cost, probs)


def exchange(x):
    return lax.all_to_all(x, "dev", split_axis=0, concat_axis=0, tiled=True)


def body(logits, route_cost, capacity, send_route, recv_piece):
    send = send_route[0].T
    pieces = jnp.swapaxes(recv_piece[:, 0], 1, 2)
    weight, probs = gather_call(logits.T, send)
    demand, slot_grad = cells_call(exchange(weight), pieces, capacity)
    grad = routes_call(exchange(slot_grad), send, route_cost.T, probs)
    return demand, grad.T


def solution(mesh):
    placed = (
        P("dev", None),
        P("dev", None),
        P("dev", None),
        P("dev", None, None),
        P(None, "dev", None, None),
    )
    return jax.shard_map(
        body,
        mesh=mesh,
        in_specs=placed,
        out_specs=(P("dev", None), P("dev", None)),
        check_vma=False,
    )
```

```python
import jax
import jax.numpy as jnp
from jax import lax
from jax.experimental import pallas as pl
from jax.experimental.pallas import tpu as pltpu
from jax.sharding import PartitionSpec as P

SHARPNESS = 2.0
BF = jnp.bfloat16
F32 = jnp.float32
CELL_DOT = 64
CELL_BACK = 4
CELL_BACK_ROWS = 64
ROUTE_DOT = 64
SUBLANES = 8
BY_PRODUCT = 32
GATHER_DOT = 8
CELL_ROWS = 64
ROUTE_ROWS = 64
PARAMS = pltpu.CompilerParams(vmem_limit_bytes=12 * 1024 * 1024)


def split(x):
    high = x.astype(BF)
    return high, (x - high.astype(F32)).astype(BF)


def iota(count, lanes):
    return lax.broadcasted_iota(jnp.int32, (count, lanes), 0)


def to_bf(x):
    return x.astype(F32).astype(BF)


def marks(mask):
    return jnp.where(mask, jnp.ones(mask.shape, BF), jnp.zeros(mask.shape, BF))


def hot(row, places):
    return places == jnp.broadcast_to(row, places.shape)


def spread(row, mask):
    return jnp.where(mask, jnp.broadcast_to(row, mask.shape), jnp.zeros(mask.shape, BF))


def pick(found, row, places):
    return jnp.sum(jnp.where(hot(row, places), found, 0.0), axis=0, keepdims=True)


def contract(left, right):
    return lax.dot_general(left, right, (((1,), (1,)), ((), ())), preferred_element_type=F32)


def route_places(routes, lanes):
    net = lax.shift_right_arithmetic(routes, 5)
    cand = lax.bitwise_and(routes, 31)
    column = lax.bitwise_and(net, lanes - 1)
    row = cand + 32 * lax.shift_right_arithmetic(net, 7)
    return column, row


def fold(x, lanes):
    return jnp.concatenate([x[:, i : i + lanes] for i in range(0, x.shape[1], lanes)], axis=0)


def unfold(x, rows):
    return jnp.concatenate([x[i : i + rows] for i in range(0, x.shape[0], rows)], axis=1)


def lane_gather(table_ref, place, lanes):
    stack = []
    for t in range(table_ref.shape[0]):
        entries = jnp.broadcast_to(table_ref[t : t + 1, :], lanes.shape)
        found = jnp.take_along_axis(entries, lanes, axis=1, mode="promise_in_bounds")
        depth = 0
        while stack and stack[-1][1] == depth:
            found = jnp.where(lax.bitwise_and(place, 1 << depth) != 0, found, stack.pop()[0])
            depth += 1
        stack.append((found, depth))
    return stack[0][0]


def gather_kernel(
    logits_hbm, send_hbm, piece_hbm, capacity_hbm, cost_hbm,
    weight_ref, prob_ref, send_ref, piece_ref, capacity_ref, cost_ref,
    logits_ref, table_ref, held_ref, sems,
):
    slots, owners = send_ref.shape
    sources = (logits_hbm, send_hbm, piece_hbm.at[pl.ds(1, 3)], capacity_hbm, cost_hbm)
    places = (logits_ref, send_ref, piece_ref, capacity_ref, cost_ref)
    copies = [pltpu.make_async_copy(x, y, sems.at[n]) for n, (x, y) in enumerate(zip(sources, places))]
    for copy in copies:
        copy.start()
    copies[0].wait()
    scores = logits_ref[...]
    powers = jnp.exp(scores - jnp.max(scores, axis=0, keepdims=True))
    probs = powers / jnp.sum(powers, axis=0, keepdims=True)
    prob_ref[...] = probs
    table_ref[...] = fold(probs, owners)
    copies[1].wait()
    column, row = route_places(send_ref[...], owners)
    high = table_ref.shape[0]
    cut = slots - BY_PRODUCT
    folded = table_ref[...]
    parts = jnp.concatenate(split(folded), axis=0)
    column_bf = to_bf(column[cut:])
    column_places = to_bf(iota(owners, owners))
    places = iota(high, owners)
    picked = []
    for k in range(0, BY_PRODUCT, GATHER_DOT):
        hots = [marks(hot(column_bf[j : j + 1], column_places)) for j in range(k, k + GATHER_DOT)]
        found = jnp.dot(parts, jnp.concatenate(hots, axis=1), preferred_element_type=F32)
        found = found[:high] + found[high:]
        for j in range(k, k + GATHER_DOT):
            part = found[:, (j - k) * owners : (j - k + 1) * owners]
            picked.append(pick(part, row[cut + j : cut + j + 1], places))
    held_ref[cut:, :] = jnp.concatenate(picked, axis=0)
    for base in range(0, cut, SUBLANES):
        lanes, place = column[base : base + SUBLANES], row[base : base + SUBLANES]
        found = lane_gather(table_ref, place, lanes)
        held_ref[base : base + SUBLANES, :] = jnp.where(place >= 0, found, 0.0)
    weight_ref[...] = held_ref[...].T
    for copy in copies[2:]:
        copy.wait()


def cells_kernel(weight_ref, piece_ref, capacity_ref, demand_ref, cover_ref, table_ref, held_ref):
    slots, sources = held_ref.shape
    tiles, cells = capacity_ref.shape
    held_ref[...] = weight_ref[...].T
    tile_places = to_bf(iota(tiles, sources))
    cell_places = to_bf(iota(cells, sources))
    width = CELL_ROWS * sources

    def add(i, total):
        base = pl.multiple_of(i * CELL_ROWS, CELL_ROWS)
        tile = to_bf(piece_ref[0, pl.ds(base, CELL_ROWS), :])
        first = piece_ref[1, pl.ds(base, CELL_ROWS), :]
        stop = to_bf(first + piece_ref[2, pl.ds(base, CELL_ROWS), :])
        first = to_bf(first)
        parts = split(held_ref[pl.ds(base, CELL_ROWS), :])
        for k in range(0, CELL_ROWS, CELL_DOT):
            lefts, rights = [], []
            for j in range(k, k + CELL_DOT):
                mask = hot(tile[j : j + 1], tile_places)
                lefts.append(jnp.concatenate([spread(part[j : j + 1], mask) for part in parts], axis=0))
                inside = jnp.logical_and(
                    cell_places >= jnp.broadcast_to(first[j : j + 1], cell_places.shape),
                    cell_places < jnp.broadcast_to(stop[j : j + 1], cell_places.shape),
                )
                rights.append(marks(inside))
                cover_ref[:, pl.ds(pl.multiple_of(i * width + j * sources, sources), sources)] = rights[-1]
            total = total + contract(jnp.concatenate(lefts, axis=1), jnp.concatenate(rights, axis=1))
        return total

    total = lax.fori_loop(0, slots // CELL_ROWS, add, jnp.zeros((2 * tiles, cells), F32))
    demand = total[:tiles] + total[tiles:]
    demand_ref[...] = demand
    pressure = jax.nn.sigmoid(SHARPNESS * (demand - capacity_ref[...].astype(F32)))
    table_ref[...] = jnp.concatenate(split(pressure), axis=0)


def slots_kernel(piece_ref, cover_ref, table_ref, demand_ref, grad_ref, demand_hbm, back_ref, sem):
    demand_out = pltpu.make_async_copy(demand_ref, demand_hbm, sem)
    demand_out.start()
    slots, sources = back_ref.shape
    tiles, cells = demand_ref.shape
    table = table_ref[...]
    places = iota(tiles, sources)

    def gather(i, carry):
        base = pl.multiple_of(i * CELL_BACK_ROWS, CELL_BACK_ROWS)
        tile = piece_ref[0, pl.ds(base, CELL_BACK_ROWS), :]
        picked = []
        for k in range(0, CELL_BACK_ROWS, CELL_BACK):
            cover = cover_ref[:, pl.ds(pl.multiple_of((base + k) * sources, sources), CELL_BACK * sources)]
            found = jnp.dot(table, cover, preferred_element_type=F32)
            found = found[:tiles] + found[tiles:]
            for j in range(k, k + CELL_BACK):
                part = found[:, (j - k) * sources : (j - k + 1) * sources]
                picked.append(pick(part, tile[j : j + 1], places))
        back_ref[pl.ds(base, CELL_BACK_ROWS), :] = jnp.concatenate(picked, axis=0)
        return carry

    lax.fori_loop(0, slots // CELL_BACK_ROWS, gather, 0)
    grad_ref[...] = back_ref[...].T
    demand_out.wait()


def routes_kernel(grad_ref, send_ref, cost_ref, prob_ref, out_ref, held_ref):
    cands, nets = prob_ref.shape
    slots, owners = send_ref.shape
    rows = cands * nets // owners
    held_ref[...] = grad_ref[...].T
    columns = to_bf(iota(owners, owners))
    places = to_bf(iota(rows, owners))

    def step(i, total):
        base = pl.multiple_of(i * ROUTE_ROWS, ROUTE_ROWS)
        column, row = route_places(send_ref[pl.ds(base, ROUTE_ROWS), :], owners)
        column, row = to_bf(column), to_bf(row)
        parts = split(held_ref[pl.ds(base, ROUTE_ROWS), :])
        for k in range(0, ROUTE_ROWS, ROUTE_DOT):
            lefts, rights = [], []
            for j in range(k, k + ROUTE_DOT):
                mask = hot(row[j : j + 1], places)
                lefts.append(jnp.concatenate([spread(part[j : j + 1], mask) for part in parts], axis=0))
                rights.append(marks(hot(column[j : j + 1], columns)))
            total = total + contract(jnp.concatenate(lefts, axis=1), jnp.concatenate(rights, axis=1))
        return total

    total = lax.fori_loop(0, slots // ROUTE_ROWS, step, jnp.zeros((2 * rows, owners), F32))
    probs = prob_ref[...]
    route_grad = cost_ref[...] + unfold(total[:rows] + total[rows:], cands)
    expected = jnp.sum(probs * route_grad, axis=0, keepdims=True)
    out_ref[...] = probs * (route_grad - expected)


def in_vmem(count):
    return [pl.BlockSpec(memory_space=pltpu.VMEM)] * count


def in_hbm(count):
    return [pl.BlockSpec(memory_space=pltpu.HBM)] * count


def gather_call(logits, send, pieces, capacity, route_cost):
    cands, nets = logits.shape
    slots, peers = send.shape
    arrays = (logits, send, pieces, capacity, route_cost)
    return pl.pallas_call(
        gather_kernel,
        out_shape=(
            jax.ShapeDtypeStruct((peers, slots), F32),
            jax.ShapeDtypeStruct((cands, nets), F32),
            jax.ShapeDtypeStruct(send.shape, send.dtype),
            jax.ShapeDtypeStruct((3, slots, peers), pieces.dtype),
            jax.ShapeDtypeStruct(capacity.shape, capacity.dtype),
            jax.ShapeDtypeStruct((cands, nets), F32),
        ),
        in_specs=in_hbm(5),
        out_specs=tuple(in_vmem(6)),
        compiler_params=PARAMS,
        scratch_shapes=[
            pltpu.VMEM((cands, nets), F32),
            pltpu.VMEM((cands * nets // peers, peers), F32),
            pltpu.VMEM((slots, peers), F32),
            pltpu.SemaphoreType.DMA((5,)),
        ],
    )(*[pltpu.with_memory_space_constraint(x, pltpu.HBM) for x in arrays])


def cells_call(weight, pieces, capacity):
    tiles, cells = capacity.shape
    peers, slots = weight.shape
    by_slot = pltpu.VMEM((slots, peers), F32)
    demand, cover, table = pl.pallas_call(
        cells_kernel,
        out_shape=(
            jax.ShapeDtypeStruct((tiles, cells), F32),
            jax.ShapeDtypeStruct((cells, slots * peers), BF),
            jax.ShapeDtypeStruct((2 * tiles, cells), BF),
        ),
        in_specs=in_vmem(3),
        out_specs=tuple(in_vmem(3)),
        compiler_params=PARAMS,
        scratch_shapes=[by_slot],
    )(weight, pieces, capacity)
    slot_grad, demand = pl.pallas_call(
        slots_kernel,
        out_shape=(jax.ShapeDtypeStruct((peers, slots), F32), jax.ShapeDtypeStruct((tiles, cells), F32)),
        in_specs=in_vmem(4),
        out_specs=tuple(in_vmem(1) + in_hbm(1)),
        compiler_params=PARAMS,
        scratch_shapes=[by_slot, pltpu.SemaphoreType.DMA],
    )(pieces, cover, table, demand)
    return demand, slot_grad


def routes_call(slot_grad, send, route_cost, probs):
    return pl.pallas_call(
        routes_kernel,
        out_shape=jax.ShapeDtypeStruct(probs.shape, F32),
        in_specs=in_vmem(4),
        out_specs=pl.BlockSpec(memory_space=pltpu.VMEM),
        compiler_params=PARAMS,
        scratch_shapes=[pltpu.VMEM(send.shape, F32)],
    )(slot_grad, send, route_cost, probs)


def exchange(x):
    return lax.all_to_all(x, "dev", split_axis=0, concat_axis=0, tiled=True)


def body(logits, route_cost, capacity, send_route, recv_piece):
    pieces = jnp.swapaxes(recv_piece[:, 0], 1, 2)
    weight, probs, send, pieces, capacity, cost = gather_call(
        logits.T, send_route[0].T, pieces, capacity, route_cost.T
    )
    demand, slot_grad = cells_call(exchange(weight), pieces, capacity)
    grad = routes_call(exchange(slot_grad), send, cost, probs)
    return demand, grad.T


def solution(mesh):
    placed = (
        P("dev", None),
        P("dev", None),
        P("dev", None),
        P("dev", None, None),
        P(None, "dev", None, None),
    )
    return jax.shard_map(
        body,
        mesh=mesh,
        in_specs=placed,
        out_specs=(P("dev", None), P("dev", None)),
        check_vma=False,
    )
```

```python
import jax
import jax.numpy as jnp
from jax import lax
from jax.experimental import pallas as pl
from jax.experimental.pallas import tpu as pltpu
from jax.sharding import PartitionSpec as P

SHARPNESS = 2.0
BF = jnp.bfloat16
F32 = jnp.float32
SUBLANES = 8
BY_PRODUCT = 32
PRODUCT_ROWS = 4
PARAMS = pltpu.CompilerParams(vmem_limit_bytes=12 * 1024 * 1024)


def split(x):
    high = x.astype(BF)
    return high, (x - high.astype(F32)).astype(BF)


def iota(count, lanes):
    return lax.broadcasted_iota(jnp.int32, (count, lanes), 0)


def to_bf(x):
    return x.astype(F32).astype(BF)


def marks(mask):
    return jnp.where(mask, jnp.ones(mask.shape, BF), jnp.zeros(mask.shape, BF))


def hot(row, places):
    return places == jnp.broadcast_to(row, places.shape)


def spread(row, mask):
    return jnp.where(mask, jnp.broadcast_to(row, mask.shape), jnp.zeros(mask.shape, BF))


def pick(found, row, places):
    return jnp.sum(jnp.where(hot(row, places), found, 0.0), axis=0, keepdims=True)


def contract(left, right):
    return lax.dot_general(left, right, (((1,), (1,)), ((), ())), preferred_element_type=F32)


def route_places(routes, lanes):
    net = lax.shift_right_arithmetic(routes, 5)
    cand = lax.bitwise_and(routes, 31)
    column = lax.bitwise_and(net, lanes - 1)
    row = cand + 32 * lax.shift_right_arithmetic(net, 7)
    return column, row


def fold(x, lanes):
    return jnp.concatenate([x[:, i : i + lanes] for i in range(0, x.shape[1], lanes)], axis=0)


def unfold(x, rows):
    return jnp.concatenate([x[i : i + rows] for i in range(0, x.shape[0], rows)], axis=1)


def lane_gather(table_ref, place, lanes):
    stack = []
    for t in range(table_ref.shape[0]):
        entries = jnp.broadcast_to(table_ref[t : t + 1, :], lanes.shape)
        found = jnp.take_along_axis(entries, lanes, axis=1, mode="promise_in_bounds")
        depth = 0
        while stack and stack[-1][1] == depth:
            found = jnp.where(lax.bitwise_and(place, 1 << depth) != 0, found, stack.pop()[0])
            depth += 1
        stack.append((found, depth))
    return stack[0][0]


def gather_kernel(
    logits_hbm, send_hbm, piece_hbm, capacity_hbm, cost_hbm,
    weight_ref, prob_ref, send_ref, piece_ref, capacity_ref, cost_ref,
    logits_ref, table_ref, held_ref, sems,
):
    slots, owners = send_ref.shape
    sources = (logits_hbm, send_hbm, piece_hbm.at[pl.ds(1, 3)], capacity_hbm, cost_hbm)
    places = (logits_ref, send_ref, piece_ref, capacity_ref, cost_ref)
    copies = [pltpu.make_async_copy(x, y, sems.at[n]) for n, (x, y) in enumerate(zip(sources, places))]
    for copy in copies:
        copy.start()
    copies[0].wait()
    scores = logits_ref[...]
    powers = jnp.exp(scores - jnp.max(scores, axis=0, keepdims=True))
    probs = powers / jnp.sum(powers, axis=0, keepdims=True)
    prob_ref[...] = probs
    table_ref[...] = fold(probs, owners)
    copies[1].wait()
    column, row = route_places(send_ref[...], owners)
    high = table_ref.shape[0]
    cut = slots - BY_PRODUCT
    folded = table_ref[...]
    parts = jnp.concatenate(split(folded), axis=0)
    column_bf = to_bf(column[cut:])
    column_places = to_bf(iota(owners, owners))
    places = iota(high, owners)
    picked = []
    for k in range(0, BY_PRODUCT, PRODUCT_ROWS):
        hots = [marks(hot(column_bf[j : j + 1], column_places)) for j in range(k, k + PRODUCT_ROWS)]
        found = jnp.dot(parts, jnp.concatenate(hots, axis=1), preferred_element_type=F32)
        found = found[:high] + found[high:]
        for j in range(k, k + PRODUCT_ROWS):
            part = found[:, (j - k) * owners : (j - k + 1) * owners]
            picked.append(pick(part, row[cut + j : cut + j + 1], places))
    held_ref[cut:, :] = jnp.concatenate(picked, axis=0)
    for base in range(0, cut, SUBLANES):
        lanes, place = column[base : base + SUBLANES], row[base : base + SUBLANES]
        found = lane_gather(table_ref, place, lanes)
        held_ref[base : base + SUBLANES, :] = jnp.where(place >= 0, found, 0.0)
    weight_ref[...] = held_ref[...].T
    for copy in copies[2:]:
        copy.wait()


def scattered(row, values, high):
    mask = hot(row, to_bf(iota(high, row.shape[1])))
    return jnp.concatenate([spread(value, mask) for value in values], axis=0)


def cells_kernel(weight_ref, piece_ref, capacity_ref, demand_ref, cover_ref, table_ref):
    tiles, cells = capacity_ref.shape
    sources, slots = weight_ref.shape
    parts = split(weight_ref[...].T)
    tile = to_bf(piece_ref[0])
    first = to_bf(piece_ref[1])
    stop = to_bf(piece_ref[1] + piece_ref[2])
    places = to_bf(iota(cells, sources))
    lefts, rights = [], []
    for j in range(slots):
        one = slice(j, j + 1)
        lefts.append(scattered(tile[one], [part[one] for part in parts], tiles))
        after = places >= jnp.broadcast_to(first[one], places.shape)
        before = places < jnp.broadcast_to(stop[one], places.shape)
        rights.append(marks(jnp.logical_and(after, before)))
        cover_ref[:, j * sources : (j + 1) * sources] = rights[-1]
    total = contract(jnp.concatenate(lefts, axis=1), jnp.concatenate(rights, axis=1))
    demand = total[:tiles] + total[tiles:]
    demand_ref[...] = demand
    pressure = jax.nn.sigmoid(SHARPNESS * (demand - capacity_ref[...].astype(F32)))
    table_ref[...] = jnp.concatenate(split(pressure), axis=0)


def slots_kernel(piece_ref, cover_ref, table_ref, demand_ref, grad_ref, demand_hbm, sem):
    demand_out = pltpu.make_async_copy(demand_ref, demand_hbm, sem)
    demand_out.start()
    tiles = demand_ref.shape[0]
    sources, slots = grad_ref.shape
    places = iota(tiles, sources)
    rows = []
    for k in range(0, slots, PRODUCT_ROWS):
        found = jnp.dot(
            table_ref[...], cover_ref[:, k * sources : (k + PRODUCT_ROWS) * sources], preferred_element_type=F32
        )
        found = found[:tiles] + found[tiles:]
        for j in range(PRODUCT_ROWS):
            part = found[:, j * sources : (j + 1) * sources]
            rows.append(pick(part, piece_ref[0, k + j : k + j + 1, :], places))
    grad_ref[...] = jnp.concatenate(rows, axis=0).T
    demand_out.wait()


def routes_kernel(grad_ref, send_ref, cost_ref, prob_ref, out_ref):
    cands, nets = prob_ref.shape
    slots, owners = send_ref.shape
    high = cands * nets // owners
    parts = split(grad_ref[...].T)
    column, row = route_places(send_ref[...], owners)
    column, row = to_bf(column), to_bf(row)
    places = to_bf(iota(owners, owners))
    lefts, rights = [], []
    for j in range(slots):
        one = slice(j, j + 1)
        lefts.append(scattered(row[one], [part[one] for part in parts], high))
        rights.append(marks(hot(column[one], places)))
    total = contract(jnp.concatenate(lefts, axis=1), jnp.concatenate(rights, axis=1))
    probs = prob_ref[...]
    route_grad = cost_ref[...] + unfold(total[:high] + total[high:], cands)
    expected = jnp.sum(probs * route_grad, axis=0, keepdims=True)
    out_ref[...] = probs * (route_grad - expected)


def in_vmem(count):
    return [pl.BlockSpec(memory_space=pltpu.VMEM)] * count


def in_hbm(count):
    return [pl.BlockSpec(memory_space=pltpu.HBM)] * count


def gather_call(logits, send, pieces, capacity, route_cost):
    cands, nets = logits.shape
    slots, peers = send.shape
    arrays = (logits, send, pieces, capacity, route_cost)
    return pl.pallas_call(
        gather_kernel,
        out_shape=(
            jax.ShapeDtypeStruct((peers, slots), F32),
            jax.ShapeDtypeStruct((cands, nets), F32),
            jax.ShapeDtypeStruct(send.shape, send.dtype),
            jax.ShapeDtypeStruct((3, slots, peers), pieces.dtype),
            jax.ShapeDtypeStruct(capacity.shape, capacity.dtype),
            jax.ShapeDtypeStruct((cands, nets), F32),
        ),
        in_specs=in_hbm(5),
        out_specs=tuple(in_vmem(6)),
        compiler_params=PARAMS,
        scratch_shapes=[
            pltpu.VMEM((cands, nets), F32),
            pltpu.VMEM((cands * nets // peers, peers), F32),
            pltpu.VMEM((slots, peers), F32),
            pltpu.SemaphoreType.DMA((5,)),
        ],
    )(*[pltpu.with_memory_space_constraint(x, pltpu.HBM) for x in arrays])


def cells_call(weight, pieces, capacity):
    tiles, cells = capacity.shape
    peers, slots = weight.shape
    demand, cover, table = pl.pallas_call(
        cells_kernel,
        out_shape=(
            jax.ShapeDtypeStruct((tiles, cells), F32),
            jax.ShapeDtypeStruct((cells, slots * peers), BF),
            jax.ShapeDtypeStruct((2 * tiles, cells), BF),
        ),
        in_specs=in_vmem(3),
        out_specs=tuple(in_vmem(3)),
        compiler_params=PARAMS,
    )(weight, pieces, capacity)
    slot_grad, demand = pl.pallas_call(
        slots_kernel,
        out_shape=(jax.ShapeDtypeStruct((peers, slots), F32), jax.ShapeDtypeStruct((tiles, cells), F32)),
        in_specs=in_vmem(4),
        out_specs=tuple(in_vmem(1) + in_hbm(1)),
        compiler_params=PARAMS,
        scratch_shapes=[pltpu.SemaphoreType.DMA],
    )(pieces, cover, table, demand)
    return demand, slot_grad


def routes_call(slot_grad, send, route_cost, probs):
    return pl.pallas_call(
        routes_kernel,
        out_shape=jax.ShapeDtypeStruct(probs.shape, F32),
        in_specs=in_vmem(4),
        out_specs=pl.BlockSpec(memory_space=pltpu.VMEM),
        compiler_params=PARAMS,
    )(slot_grad, send, route_cost, probs)


def exchange(x):
    return lax.all_to_all(x, "dev", split_axis=0, concat_axis=0, tiled=True)


def body(logits, route_cost, capacity, send_route, recv_piece):
    pieces = jnp.swapaxes(recv_piece[:, 0], 1, 2)
    weight, probs, send, pieces, capacity, cost = gather_call(
        logits.T, send_route[0].T, pieces, capacity, route_cost.T
    )
    demand, slot_grad = cells_call(exchange(weight), pieces, capacity)
    grad = routes_call(exchange(slot_grad), send, cost, probs)
    return demand, grad.T


def solution(mesh):
    placed = (
        P("dev", None),
        P("dev", None),
        P("dev", None),
        P("dev", None, None),
        P(None, "dev", None, None),
    )
    return jax.shard_map(
        body,
        mesh=mesh,
        in_specs=placed,
        out_specs=(P("dev", None), P("dev", None)),
        check_vma=False,
    )
```

```python
import jax
import jax.numpy as jnp
from jax import lax
from jax.experimental import pallas as pl
from jax.experimental.pallas import tpu as pltpu
from jax.sharding import PartitionSpec as P

SHARPNESS = 2.0
BF = jnp.bfloat16
F32 = jnp.float32
SUBLANES = 8
BY_PRODUCT = 32
PRODUCT_ROWS = 4
BY_SUMS = 16
PARAMS = pltpu.CompilerParams(vmem_limit_bytes=12 * 1024 * 1024)


def split(x):
    high = x.astype(BF)
    return high, (x - high.astype(F32)).astype(BF)


def iota(count, lanes):
    return lax.broadcasted_iota(jnp.int32, (count, lanes), 0)


def to_bf(x):
    return x.astype(F32).astype(BF)


def marks(mask):
    return jnp.where(mask, jnp.ones(mask.shape, BF), jnp.zeros(mask.shape, BF))


def hot(row, places):
    return places == jnp.broadcast_to(row, places.shape)


def spread(row, mask):
    return jnp.where(mask, jnp.broadcast_to(row, mask.shape), jnp.zeros(mask.shape, BF))


def pick(found, row, places):
    return jnp.sum(jnp.where(hot(row, places), found, 0.0), axis=0, keepdims=True)


def contract(left, right):
    return lax.dot_general(left, right, (((1,), (1,)), ((), ())), preferred_element_type=F32)


def route_places(routes, lanes):
    net = lax.shift_right_arithmetic(routes, 5)
    cand = lax.bitwise_and(routes, 31)
    column = lax.bitwise_and(net, lanes - 1)
    row = cand + 32 * lax.shift_right_arithmetic(net, 7)
    return column, row


def fold(x, lanes):
    return jnp.concatenate([x[:, i : i + lanes] for i in range(0, x.shape[1], lanes)], axis=0)


def unfold(x, rows):
    return jnp.concatenate([x[i : i + rows] for i in range(0, x.shape[0], rows)], axis=1)


def lane_gather(table_ref, place, lanes):
    stack = []
    for t in range(table_ref.shape[0]):
        entries = jnp.broadcast_to(table_ref[t : t + 1, :], lanes.shape)
        found = jnp.take_along_axis(entries, lanes, axis=1, mode="promise_in_bounds")
        depth = 0
        while stack and stack[-1][1] == depth:
            found = jnp.where(lax.bitwise_and(place, 1 << depth) != 0, found, stack.pop()[0])
            depth += 1
        stack.append((found, depth))
    return stack[0][0]


def gather_kernel(
    logits_hbm, send_hbm, piece_hbm, capacity_hbm, cost_hbm,
    weight_ref, prob_ref, send_ref, piece_ref, capacity_ref, cost_ref,
    logits_ref, table_ref, held_ref, sems,
):
    slots, owners = send_ref.shape
    sources = (logits_hbm, send_hbm, piece_hbm.at[pl.ds(1, 3)], capacity_hbm, cost_hbm)
    places = (logits_ref, send_ref, piece_ref, capacity_ref, cost_ref)
    copies = [pltpu.make_async_copy(x, y, sems.at[n]) for n, (x, y) in enumerate(zip(sources, places))]
    for copy in copies:
        copy.start()
    copies[0].wait()
    scores = logits_ref[...]
    powers = jnp.exp(scores - jnp.max(scores, axis=0, keepdims=True))
    probs = powers / jnp.sum(powers, axis=0, keepdims=True)
    prob_ref[...] = probs
    table_ref[...] = fold(probs, owners)
    copies[1].wait()
    column, row = route_places(send_ref[...], owners)
    high = table_ref.shape[0]
    cut = slots - BY_PRODUCT
    folded = table_ref[...]
    parts = jnp.concatenate(split(folded), axis=0)
    column_bf = to_bf(column[cut:])
    column_places = to_bf(iota(owners, owners))
    places = iota(high, owners)
    picked = []
    for k in range(0, BY_PRODUCT, PRODUCT_ROWS):
        hots = [marks(hot(column_bf[j : j + 1], column_places)) for j in range(k, k + PRODUCT_ROWS)]
        found = jnp.dot(parts, jnp.concatenate(hots, axis=1), preferred_element_type=F32)
        found = found[:high] + found[high:]
        for j in range(k, k + PRODUCT_ROWS):
            part = found[:, (j - k) * owners : (j - k + 1) * owners]
            picked.append(pick(part, row[cut + j : cut + j + 1], places))
    held_ref[cut:, :] = jnp.concatenate(picked, axis=0)
    for base in range(0, cut, SUBLANES):
        lanes, place = column[base : base + SUBLANES], row[base : base + SUBLANES]
        found = lane_gather(table_ref, place, lanes)
        held_ref[base : base + SUBLANES, :] = jnp.where(place >= 0, found, 0.0)
    weight_ref[...] = held_ref[...].T
    for copy in copies[2:]:
        copy.wait()


def scattered(row, values, high):
    mask = hot(row, to_bf(iota(high, row.shape[1])))
    return jnp.concatenate([spread(value, mask) for value in values], axis=0)


def cells_kernel(weight_ref, piece_ref, capacity_ref, demand_ref, cover_ref, table_ref):
    tiles, cells = capacity_ref.shape
    sources, slots = weight_ref.shape
    parts = split(weight_ref[...].T)
    tile = to_bf(piece_ref[0])
    first = to_bf(piece_ref[1])
    stop = to_bf(piece_ref[1] + piece_ref[2])
    places = to_bf(iota(cells, sources))
    lefts, rights = [], []
    for j in range(slots):
        one = slice(j, j + 1)
        lefts.append(scattered(tile[one], [part[one] for part in parts], tiles))
        after = places >= jnp.broadcast_to(first[one], places.shape)
        before = places < jnp.broadcast_to(stop[one], places.shape)
        rights.append(marks(jnp.logical_and(after, before)))
        cover_ref[:, j * sources : (j + 1) * sources] = rights[-1]
    total = contract(jnp.concatenate(lefts, axis=1), jnp.concatenate(rights, axis=1))
    demand = total[:tiles] + total[tiles:]
    demand_ref[...] = demand
    pressure = jax.nn.sigmoid(SHARPNESS * (demand - capacity_ref[...].astype(F32)))
    table_ref[...] = jnp.concatenate(split(pressure), axis=0)


def slots_kernel(piece_ref, cover_ref, table_ref, demand_ref, grad_ref, demand_hbm, upto_ref, before_ref, sem):
    demand_out = pltpu.make_async_copy(demand_ref, demand_hbm, sem)
    demand_out.start()
    tiles, cells = demand_ref.shape
    sources, slots = grad_ref.shape
    places = iota(tiles, sources)
    cut = slots - BY_SUMS
    steps = marks(iota(cells, cells) <= lax.broadcasted_iota(jnp.int32, (cells, cells), 1))
    sums = jnp.dot(table_ref[...], steps, preferred_element_type=F32)
    upto = sums[:tiles] + sums[tiles:]
    upto_ref[...] = upto
    before_ref[...] = upto - (table_ref[:tiles].astype(F32) + table_ref[tiles:].astype(F32))
    rows = []
    for k in range(0, cut, PRODUCT_ROWS):
        found = jnp.dot(
            table_ref[...], cover_ref[:, k * sources : (k + PRODUCT_ROWS) * sources], preferred_element_type=F32
        )
        found = found[:tiles] + found[tiles:]
        for j in range(PRODUCT_ROWS):
            part = found[:, j * sources : (j + 1) * sources]
            rows.append(pick(part, piece_ref[0, k + j : k + j + 1, :], places))
    for k in range(cut, slots, SUBLANES):
        tile, first, count = (piece_ref[n, k : k + SUBLANES, :] for n in range(3))
        last = jnp.maximum(first + count - 1, 0)
        inside = lane_gather(upto_ref, tile, last) - lane_gather(before_ref, tile, first)
        rows.append(jnp.where(count > 0, inside, 0.0))
    grad_ref[...] = jnp.concatenate(rows, axis=0).T
    demand_out.wait()


def routes_kernel(grad_ref, send_ref, cost_ref, prob_ref, out_ref):
    cands, nets = prob_ref.shape
    slots, owners = send_ref.shape
    high = cands * nets // owners
    parts = split(grad_ref[...].T)
    column, row = route_places(send_ref[...], owners)
    column, row = to_bf(column), to_bf(row)
    places = to_bf(iota(owners, owners))
    lefts, rights = [], []
    for j in range(slots):
        one = slice(j, j + 1)
        lefts.append(scattered(row[one], [part[one] for part in parts], high))
        rights.append(marks(hot(column[one], places)))
    total = contract(jnp.concatenate(lefts, axis=1), jnp.concatenate(rights, axis=1))
    probs = prob_ref[...]
    route_grad = cost_ref[...] + unfold(total[:high] + total[high:], cands)
    expected = jnp.sum(probs * route_grad, axis=0, keepdims=True)
    out_ref[...] = probs * (route_grad - expected)


def in_vmem(count):
    return [pl.BlockSpec(memory_space=pltpu.VMEM)] * count


def in_hbm(count):
    return [pl.BlockSpec(memory_space=pltpu.HBM)] * count


def gather_call(logits, send, pieces, capacity, route_cost):
    cands, nets = logits.shape
    slots, peers = send.shape
    arrays = (logits, send, pieces, capacity, route_cost)
    return pl.pallas_call(
        gather_kernel,
        out_shape=(
            jax.ShapeDtypeStruct((peers, slots), F32),
            jax.ShapeDtypeStruct((cands, nets), F32),
            jax.ShapeDtypeStruct(send.shape, send.dtype),
            jax.ShapeDtypeStruct((3, slots, peers), pieces.dtype),
            jax.ShapeDtypeStruct(capacity.shape, capacity.dtype),
            jax.ShapeDtypeStruct((cands, nets), F32),
        ),
        in_specs=in_hbm(5),
        out_specs=tuple(in_vmem(6)),
        compiler_params=PARAMS,
        scratch_shapes=[
            pltpu.VMEM((cands, nets), F32),
            pltpu.VMEM((cands * nets // peers, peers), F32),
            pltpu.VMEM((slots, peers), F32),
            pltpu.SemaphoreType.DMA((5,)),
        ],
    )(*[pltpu.with_memory_space_constraint(x, pltpu.HBM) for x in arrays])


def cells_call(weight, pieces, capacity):
    tiles, cells = capacity.shape
    peers, slots = weight.shape
    demand, cover, table = pl.pallas_call(
        cells_kernel,
        out_shape=(
            jax.ShapeDtypeStruct((tiles, cells), F32),
            jax.ShapeDtypeStruct((cells, slots * peers), BF),
            jax.ShapeDtypeStruct((2 * tiles, cells), BF),
        ),
        in_specs=in_vmem(3),
        out_specs=tuple(in_vmem(3)),
        compiler_params=PARAMS,
    )(weight, pieces, capacity)
    slot_grad, demand = pl.pallas_call(
        slots_kernel,
        out_shape=(jax.ShapeDtypeStruct((peers, slots), F32), jax.ShapeDtypeStruct((tiles, cells), F32)),
        in_specs=in_vmem(4),
        out_specs=tuple(in_vmem(1) + in_hbm(1)),
        compiler_params=PARAMS,
        scratch_shapes=[pltpu.VMEM((tiles, cells), F32), pltpu.VMEM((tiles, cells), F32), pltpu.SemaphoreType.DMA],
    )(pieces, cover, table, demand)
    return demand, slot_grad


def routes_call(slot_grad, send, route_cost, probs):
    return pl.pallas_call(
        routes_kernel,
        out_shape=jax.ShapeDtypeStruct(probs.shape, F32),
        in_specs=in_vmem(4),
        out_specs=pl.BlockSpec(memory_space=pltpu.VMEM),
        compiler_params=PARAMS,
    )(slot_grad, send, route_cost, probs)


def exchange(x):
    return lax.all_to_all(x, "dev", split_axis=0, concat_axis=0, tiled=True)


def body(logits, route_cost, capacity, send_route, recv_piece):
    pieces = jnp.swapaxes(recv_piece[:, 0], 1, 2)
    weight, probs, send, pieces, capacity, cost = gather_call(
        logits.T, send_route[0].T, pieces, capacity, route_cost.T
    )
    demand, slot_grad = cells_call(exchange(weight), pieces, capacity)
    grad = routes_call(exchange(slot_grad), send, cost, probs)
    return demand, grad.T


def solution(mesh):
    placed = (
        P("dev", None),
        P("dev", None),
        P("dev", None),
        P("dev", None, None),
        P(None, "dev", None, None),
    )
    return jax.shard_map(
        body,
        mesh=mesh,
        in_specs=placed,
        out_specs=(P("dev", None), P("dev", None)),
        check_vma=False,
    )
```

```python
import jax
import jax.numpy as jnp
from jax import lax
from jax.experimental import pallas as pl
from jax.experimental.pallas import tpu as pltpu
from jax.sharding import PartitionSpec as P

SHARPNESS = 2.0
BF = jnp.bfloat16
F32 = jnp.float32
SUBLANES = 8
BY_PRODUCT = 32
PRODUCT_ROWS = 4
BY_SUMS = 16
PARAMS = pltpu.CompilerParams(vmem_limit_bytes=12 * 1024 * 1024)


def split(x):
    high = x.astype(BF)
    return high, (x - high.astype(F32)).astype(BF)


def iota(count, lanes):
    return lax.broadcasted_iota(jnp.int32, (count, lanes), 0)


def to_bf(x):
    return x.astype(F32).astype(BF)


def marks(mask):
    return jnp.where(mask, jnp.ones(mask.shape, BF), jnp.zeros(mask.shape, BF))


def hot(row, places):
    return places == jnp.broadcast_to(row, places.shape)


def spread(row, mask):
    return jnp.where(mask, jnp.broadcast_to(row, mask.shape), jnp.zeros(mask.shape, BF))


def pick(found, row, places):
    return jnp.sum(jnp.where(hot(row, places), found, 0.0), axis=0, keepdims=True)


def contract(left, right):
    return lax.dot_general(left, right, (((1,), (1,)), ((), ())), preferred_element_type=F32)


def route_places(routes, lanes):
    net = lax.shift_right_arithmetic(routes, 5)
    cand = lax.bitwise_and(routes, 31)
    column = lax.bitwise_and(net, lanes - 1)
    row = cand + 32 * lax.shift_right_arithmetic(net, 7)
    return column, row


def fold(x, lanes):
    return jnp.concatenate([x[:, i : i + lanes] for i in range(0, x.shape[1], lanes)], axis=0)


def unfold(x, rows):
    return jnp.concatenate([x[i : i + rows] for i in range(0, x.shape[0], rows)], axis=1)


def lane_gather(table_ref, place, lanes):
    stack = []
    for t in range(table_ref.shape[0]):
        entries = jnp.broadcast_to(table_ref[t : t + 1, :], lanes.shape)
        found = jnp.take_along_axis(entries, lanes, axis=1, mode="promise_in_bounds")
        depth = 0
        while stack and stack[-1][1] == depth:
            found = jnp.where(lax.bitwise_and(place, 1 << depth) != 0, found, stack.pop()[0])
            depth += 1
        stack.append((found, depth))
    return stack[0][0]


def gather_kernel(
    logits_hbm, send_hbm, piece_hbm, capacity_hbm, cost_hbm,
    weight_ref, prob_ref, send_ref, piece_ref, capacity_ref, cost_ref,
    logits_ref, table_ref, sems,
):
    slots, owners = send_ref.shape
    sources = (logits_hbm, send_hbm, piece_hbm.at[pl.ds(1, 3)], capacity_hbm, cost_hbm)
    places = (logits_ref, send_ref, piece_ref, capacity_ref, cost_ref)
    copies = [pltpu.make_async_copy(x, y, sems.at[n]) for n, (x, y) in enumerate(zip(sources, places))]
    for copy in copies:
        copy.start()
    copies[0].wait()
    scores = logits_ref[...]
    powers = jnp.exp(scores - jnp.max(scores, axis=0, keepdims=True))
    probs = powers / jnp.sum(powers, axis=0, keepdims=True)
    prob_ref[...] = probs
    table_ref[...] = fold(probs, owners)
    copies[1].wait()
    column, row = route_places(send_ref[...], owners)
    high = table_ref.shape[0]
    cut = slots - BY_PRODUCT
    folded = table_ref[...]
    parts = jnp.concatenate(split(folded), axis=0)
    column_bf = to_bf(column[cut:])
    column_places = to_bf(iota(owners, owners))
    places = iota(high, owners)
    picked = []
    for k in range(0, BY_PRODUCT, PRODUCT_ROWS):
        hots = [marks(hot(column_bf[j : j + 1], column_places)) for j in range(k, k + PRODUCT_ROWS)]
        found = jnp.dot(parts, jnp.concatenate(hots, axis=1), preferred_element_type=F32)
        found = found[:high] + found[high:]
        for j in range(k, k + PRODUCT_ROWS):
            part = found[:, (j - k) * owners : (j - k + 1) * owners]
            picked.append(pick(part, row[cut + j : cut + j + 1], places))
    taken = []
    for base in range(0, cut, SUBLANES):
        lanes, place = column[base : base + SUBLANES], row[base : base + SUBLANES]
        found = lane_gather(table_ref, place, lanes)
        taken.append(jnp.where(place >= 0, found, 0.0))
    weight_ref[...] = jnp.concatenate(taken + picked, axis=0).T
    for copy in copies[2:]:
        copy.wait()


def scattered(row, values, high):
    mask = hot(row, to_bf(iota(high, row.shape[1])))
    return jnp.concatenate([spread(value, mask) for value in values], axis=0)


def cells_kernel(weight_ref, piece_ref, capacity_ref, demand_ref, cover_ref, table_ref):
    tiles, cells = capacity_ref.shape
    sources, slots = weight_ref.shape
    parts = split(weight_ref[...].T)
    tile = to_bf(piece_ref[0])
    first = to_bf(piece_ref[1])
    stop = to_bf(piece_ref[1] + piece_ref[2])
    places = to_bf(iota(cells, sources))
    lefts, rights = [], []
    for j in range(slots):
        one = slice(j, j + 1)
        lefts.append(scattered(tile[one], [part[one] for part in parts], tiles))
        after = places >= jnp.broadcast_to(first[one], places.shape)
        before = places < jnp.broadcast_to(stop[one], places.shape)
        rights.append(marks(jnp.logical_and(after, before)))
        cover_ref[:, j * sources : (j + 1) * sources] = rights[-1]
    total = contract(jnp.concatenate(lefts, axis=1), jnp.concatenate(rights, axis=1))
    demand = total[:tiles] + total[tiles:]
    demand_ref[...] = demand
    pressure = jax.nn.sigmoid(SHARPNESS * (demand - capacity_ref[...].astype(F32)))
    table_ref[...] = jnp.concatenate(split(pressure), axis=0)


def slots_kernel(piece_ref, cover_ref, table_ref, demand_ref, grad_ref, demand_hbm, upto_ref, before_ref, sem):
    demand_out = pltpu.make_async_copy(demand_ref, demand_hbm, sem)
    demand_out.start()
    tiles, cells = demand_ref.shape
    sources, slots = grad_ref.shape
    places = iota(tiles, sources)
    cut = slots - BY_SUMS
    steps = marks(iota(cells, cells) <= lax.broadcasted_iota(jnp.int32, (cells, cells), 1))
    sums = jnp.dot(table_ref[...], steps, preferred_element_type=F32)
    upto = sums[:tiles] + sums[tiles:]
    upto_ref[...] = upto
    before_ref[...] = upto - (table_ref[:tiles].astype(F32) + table_ref[tiles:].astype(F32))
    rows = []
    for k in range(0, cut, PRODUCT_ROWS):
        found = jnp.dot(
            table_ref[...], cover_ref[:, k * sources : (k + PRODUCT_ROWS) * sources], preferred_element_type=F32
        )
        found = found[:tiles] + found[tiles:]
        for j in range(PRODUCT_ROWS):
            part = found[:, j * sources : (j + 1) * sources]
            rows.append(pick(part, piece_ref[0, k + j : k + j + 1, :], places))
    for k in range(cut, slots, SUBLANES):
        tile, first, count = (piece_ref[n, k : k + SUBLANES, :] for n in range(3))
        last = jnp.maximum(first + count - 1, 0)
        inside = lane_gather(upto_ref, tile, last) - lane_gather(before_ref, tile, first)
        rows.append(jnp.where(count > 0, inside, 0.0))
    grad_ref[...] = jnp.concatenate(rows, axis=0).T
    demand_out.wait()


def routes_kernel(grad_ref, send_ref, cost_ref, prob_ref, out_ref):
    cands, nets = prob_ref.shape
    slots, owners = send_ref.shape
    high = cands * nets // owners
    parts = split(grad_ref[...].T)
    column, row = route_places(send_ref[...], owners)
    column, row = to_bf(column), to_bf(row)
    places = to_bf(iota(owners, owners))
    lefts, rights = [], []
    for j in range(slots):
        one = slice(j, j + 1)
        lefts.append(scattered(row[one], [part[one] for part in parts], high))
        rights.append(marks(hot(column[one], places)))
    total = contract(jnp.concatenate(lefts, axis=1), jnp.concatenate(rights, axis=1))
    probs = prob_ref[...]
    route_grad = cost_ref[...] + unfold(total[:high] + total[high:], cands)
    expected = jnp.sum(probs * route_grad, axis=0, keepdims=True)
    out_ref[...] = probs * (route_grad - expected)


def in_vmem(count):
    return [pl.BlockSpec(memory_space=pltpu.VMEM)] * count


def in_hbm(count):
    return [pl.BlockSpec(memory_space=pltpu.HBM)] * count


def gather_call(logits, send, pieces, capacity, route_cost):
    cands, nets = logits.shape
    slots, peers = send.shape
    arrays = (logits, send, pieces, capacity, route_cost)
    return pl.pallas_call(
        gather_kernel,
        out_shape=(
            jax.ShapeDtypeStruct((peers, slots), F32),
            jax.ShapeDtypeStruct((cands, nets), F32),
            jax.ShapeDtypeStruct(send.shape, send.dtype),
            jax.ShapeDtypeStruct((3, slots, peers), pieces.dtype),
            jax.ShapeDtypeStruct(capacity.shape, capacity.dtype),
            jax.ShapeDtypeStruct((cands, nets), F32),
        ),
        in_specs=in_hbm(5),
        out_specs=tuple(in_vmem(6)),
        compiler_params=PARAMS,
        scratch_shapes=[
            pltpu.VMEM((cands, nets), F32),
            pltpu.VMEM((cands * nets // peers, peers), F32),
            pltpu.SemaphoreType.DMA((5,)),
        ],
    )(*[pltpu.with_memory_space_constraint(x, pltpu.HBM) for x in arrays])


def cells_call(weight, pieces, capacity):
    tiles, cells = capacity.shape
    peers, slots = weight.shape
    demand, cover, table = pl.pallas_call(
        cells_kernel,
        out_shape=(
            jax.ShapeDtypeStruct((tiles, cells), F32),
            jax.ShapeDtypeStruct((cells, slots * peers), BF),
            jax.ShapeDtypeStruct((2 * tiles, cells), BF),
        ),
        in_specs=in_vmem(3),
        out_specs=tuple(in_vmem(3)),
        compiler_params=PARAMS,
    )(weight, pieces, capacity)
    slot_grad, demand = pl.pallas_call(
        slots_kernel,
        out_shape=(jax.ShapeDtypeStruct((peers, slots), F32), jax.ShapeDtypeStruct((tiles, cells), F32)),
        in_specs=in_vmem(4),
        out_specs=tuple(in_vmem(1) + in_hbm(1)),
        compiler_params=PARAMS,
        scratch_shapes=[pltpu.VMEM((tiles, cells), F32), pltpu.VMEM((tiles, cells), F32), pltpu.SemaphoreType.DMA],
    )(pieces, cover, table, demand)
    return demand, slot_grad


def routes_call(slot_grad, send, route_cost, probs):
    return pl.pallas_call(
        routes_kernel,
        out_shape=jax.ShapeDtypeStruct(probs.shape, F32),
        in_specs=in_vmem(4),
        out_specs=pl.BlockSpec(memory_space=pltpu.VMEM),
        compiler_params=PARAMS,
    )(slot_grad, send, route_cost, probs)


def exchange(x):
    return lax.all_to_all(x, "dev", split_axis=0, concat_axis=0, tiled=True)


def body(logits, route_cost, capacity, send_route, recv_piece):
    pieces = jnp.swapaxes(recv_piece[:, 0], 1, 2)
    weight, probs, send, pieces, capacity, cost = gather_call(
        logits.T, send_route[0].T, pieces, capacity, route_cost.T
    )
    demand, slot_grad = cells_call(exchange(weight), pieces, capacity)
    grad = routes_call(exchange(slot_grad), send, cost, probs)
    return demand, grad.T


def solution(mesh):
    placed = (
        P("dev", None),
        P("dev", None),
        P("dev", None),
        P("dev", None, None),
        P(None, "dev", None, None),
    )
    return jax.shard_map(
        body,
        mesh=mesh,
        in_specs=placed,
        out_specs=(P("dev", None), P("dev", None)),
        check_vma=False,
    )
```
